32 devices in a mesh: group: 4 (over x, core), tensor: 8 (over z, y).
Axes of the slice: x: 2, y: 2, z: 4, core: 2. Of those that a mesh axis runs over, the one named last changes fastest.
Arguments:
- hidden_in: bfloat16 [8192, 1536], P(('group', 'tensor')), may hold values from -6 to 6
- request_ids: int32 [32, 256], P(('group', 'tensor')), may hold values from 0 to 3, never falling along the last dimension, each value on 1 to 128 neighbouring positions
- norm_gains: float32 [2, 1536], replicated, may hold values from 0.5 to 1.5
- query_key_value_weight: bfloat16 [1536, 3072], replicated, may hold values from -0.15625 to 0.15625
- w_out: bfloat16 [1536, 1536], replicated, may hold values from -0.15625 to 0.15625
- w_in: bfloat16 [2, 1536, 4096], P(None, None, 'tensor'), may hold values from -0.15625 to 0.15625
- w_down: bfloat16 [4096, 1536], P('tensor'), may hold values from -0.09375 to 0.09375
- prefix_cache: bfloat16 [4, 1024, 1536], P('group', 'tensor'), may hold values from -210 to 210
- prefix_owner: int32 [8], replicated, may hold values from 0 to 3
- page_dest: int32 [512, 1], P(('group', 'tensor')), may hold values from 0 to 3; in each aligned block of 16 rows (0 to 15, 16 to 31, ...) at most 8 rows name the same one
Outputs:
- hidden_out: bfloat16 [8192, 1536], P(('group', 'tensor'))
- suffix_cache: bfloat16 [4, 8, 4, 8, 16, 1536], P('group', 'tensor')
The draws below stay inside these ranges and needn't reach their ends.
Inputs may be any that keep to these rules, and one draw needn't show every extreme that they name: `request_ids`: each row numbers its requests from 0 in order of tokens, never falling, each request holding 1 to 128 tokens. `prefix_owner`: each block of the prefix cache is read from the slot of its owner only. `page_dest`: among the 16 pages of one device at most 8 have the same destination, and exactly 8 in some devices.
All inputs are finite; a program needn't handle non-finite values.
Results may differ from the reference program's by a relative error of at most 0.013.
The reference program's roundings to bfloat16 on the way count: a program that leaves them out, or rounds other values in their place, can miss the bound.
Values may be sent and summed in bfloat16 or wider, within the bound.
No kernel may reach another device: no remote copies, remote signals or barrier semaphores. Data moves between devices by JAX's collectives and lax.ppermute only.
A program may use at most 192 MiB of HBM per device.

```python
import math
import jax
import jax.numpy as jnp
import numpy as np
from jax import lax

MODEL_DIMENSION = 1536
QUERY_HEADS = 16
KEY_VALUE_HEADS = 8
HEAD_DIMENSION = 96
FF = 4096
PREFIX_TOKENS = 1024
TOK_DEV = 256
PAGE = 16
REQ_DEV = 4
MOST = 128
PAGES_DEV = 16
CAP = 8
TOKENS = 8192
N_GROUP = 4
N_TENSOR = 8


def draw_prefix_cache(key, part):
    base_key = jax.random.fold_in(key, 0)
    cache_layout = (N_GROUP, PREFIX_TOKENS, 2 * KEY_VALUE_HEADS * HEAD_DIMENSION)
    drawn = jax.random.truncated_normal(base_key, -6.0, 6.0, cache_layout, jnp.float32)
    return drawn.astype(jnp.bfloat16)


def set_ends(array, own_key, least, top_value):
    extent = array.shape
    index_at = [jax.random.randint(jax.random.fold_in(own_key, axis), (), 0, extent[axis]) for axis in range(len(extent))]
    array = array.at[tuple(index_at)].set(least)
    longest = extent.index(max(extent))
    index_at[longest] = (index_at[longest] + 1) % extent[longest]
    return array.at[tuple(index_at)].set(top_value)


def steps_of(key, shape, cuts, least, top_value):
    gain = 1.0
    for axis_at, blocks in cuts:
        draws = jax.random.uniform(jax.random.fold_in(jax.random.fold_in(key, 6), axis_at), (blocks,), jnp.float32, least / len(cuts), top_value / len(cuts))
        gain = gain * jnp.repeat(jnp.exp(draws), shape[axis_at] // blocks).reshape((-1,) + (1,) * (len(shape) - 1 - axis_at))
    return gain


def profile(amount, total, limit, slope):
    portions = [(1 << 20) // math.isqrt(rank ** slope) + 1 for rank in range(2, amount + 1)]
    rest, given = total - limit - (amount - 1), [1] * (amount - 1)
    while rest > 0:
        candidates = [i for i in range(amount - 1) if given[i] < limit]
        pool, remaining = sum([portions[i] for i in candidates]), rest
        for i in candidates:
            extra = min(limit - given[i], max(1, remaining * portions[i] // pool), rest)
            given[i] = given[i] + extra
            rest = rest - extra
    return np.array([limit] + given)


def uneven_parts(rng, count, total, reach, slope):
    if count == 2:
        one = jax.random.randint(rng, (), max(1, total - reach), min(reach, total - 1) + 1)
        return jnp.stack([one, total - one])
    tallies = jnp.asarray(profile(count, total, reach, slope), jnp.int32)
    couples = (count - 1) // 2
    donor, taker = tallies[1:1 + 2 * couples:2], tallies[2:2 + 2 * couples:2]
    room = jnp.minimum(donor - 1, reach - taker)
    shifted = jax.random.randint(jax.random.fold_in(rng, 1), (couples,), 0, 1 << 20) % (room + 1)
    tallies = tallies.at[1:1 + 2 * couples:2].set(donor - shifted).at[2:2 + 2 * couples:2].set(taker + shifted)
    return tallies[jax.random.permutation(jax.random.fold_in(rng, 2), count)]


def routed_block(key, own, number, rows, amount, top, bound, skew):
    order = jax.random.permutation(key, amount)
    heavy_load, common = portions_of(amount, rows * top, bound, skew, True), portions_of(amount, rows * top, bound, skew, False)
    places = jnp.arange(amount)

    def named(sizes, rotation):
        used = int((sizes > 0).sum())
        fixed = max(1, used // 4)
        shifted = fixed + (places - fixed + rotation * (used - fixed)) % max(1, amount - fixed)
        return jnp.zeros((amount,), jnp.int32).at[order[jnp.where(places < fixed, places, shifted)]].set(jnp.asarray(sizes, jnp.int32))

    sizes = jnp.where(number % 4 == 0, named(heavy_load, number // 4), named(common, number - number // 4 - 1))
    mixed = jax.random.permutation(jax.random.fold_in(own, 3), amount)
    source_of, taker = mixed[0:amount // 2 * 2:2], mixed[1:amount // 2 * 2:2]
    margin = jnp.minimum(sizes[source_of] - 1, bound - sizes[taker]) // 2
    margin = jnp.where((source_of == order[0]) | (taker == order[0]) | (sizes[taker] == 0), 0, jnp.maximum(margin, 0))
    shifted = jax.random.randint(jax.random.fold_in(own, 4), (amount // 2,), 0, 1 << 20) % (margin + 1)
    sizes = sizes.at[source_of].add(-shifted).at[taker].add(shifted)
    items = jnp.searchsorted(jnp.cumsum(sizes), jnp.arange(rows * top), side="right").astype(jnp.int32)
    table = items.reshape(top, rows).T
    table = table[jax.random.permutation(jax.random.fold_in(own, 1), rows)]
    rotation = jax.random.randint(jax.random.fold_in(own, 2), (rows, 1), 0, top)
    return jnp.take_along_axis(table, (jnp.arange(top)[None, :] + rotation) % top, axis=1)


def portions_of(number_of, total, limit, skew, full):
    loads = [(1 << 20) // math.isqrt(standing ** skew) + 1 for standing in range(1, number_of + 1)]
    largest = limit if full else min(limit, max(-(-total // number_of), total * loads[0] // sum(loads)))
    least = 1 if total - largest >= number_of - 1 else 0
    given, spare = [largest] + [least] * (number_of - 1), total - largest - least * (number_of - 1)
    while spare > 0:
        candidates = [i for i in range(1, number_of) if given[i] < largest] or [i for i in range(1, number_of) if given[i] < limit]
        mass, budget = sum([loads[i] for i in candidates]), spare
        for i in candidates:
            addition = min(limit - given[i], max(1, budget * loads[i] // mass), spare)
            given[i] = given[i] + addition
            spare = spare - addition
    return np.array(given)


def noise(rng, extent, width, limit, cuts=(), kind=jnp.bfloat16):
    values = width * jax.random.normal(rng, extent, jnp.float32)
    if cuts:
        values = values * steps_of(rng, extent, cuts, -0.22, 0.18)
    return jnp.clip(values, -limit, limit).astype(kind)


def setup_inputs(seed: int = 0) -> dict:
    seeds = jax.random.split(jax.random.key(seed), 11)
    hidden_in = noise(seeds[0], (TOKENS, MODEL_DIMENSION), 1.0, 6.0, ((0, 32),))
    request_ids = jax.vmap(lambda own: jnp.searchsorted(jnp.cumsum(uneven_parts(own, REQ_DEV, TOK_DEV, MOST, 1)), jnp.arange(TOK_DEV), side="right"))(jax.random.split(seeds[1], (N_GROUP * N_TENSOR))).reshape((N_GROUP * N_TENSOR, TOK_DEV)).astype(jnp.int32)
    norm_gains = jnp.clip(1.0 + 0.1 * jax.random.normal(seeds[2], (2, MODEL_DIMENSION), jnp.float32), 0.5, 1.5)
    query_key_value_weight = noise(seeds[3], (MODEL_DIMENSION, (QUERY_HEADS + 2 * KEY_VALUE_HEADS) * HEAD_DIMENSION), MODEL_DIMENSION ** -0.5, 0.15625)
    w_out = noise(seeds[4], (QUERY_HEADS * HEAD_DIMENSION, MODEL_DIMENSION), (QUERY_HEADS * HEAD_DIMENSION) ** -0.5, 0.15625)
    w_in = noise(seeds[5], (2, MODEL_DIMENSION, FF), MODEL_DIMENSION ** -0.5, 0.15625, ((2, 8),))
    w_down = noise(seeds[6], (FF, MODEL_DIMENSION), FF ** -0.5, 0.09375, ((0, 8),))
    prefix_cache = draw_prefix_cache(jax.random.fold_in(seeds[10], 71), 0)
    prefix_owner = set_ends(jax.random.randint(seeds[8], (N_TENSOR,), 0, N_GROUP), jax.random.fold_in(seeds[8], 1), 0, N_GROUP - 1).astype(jnp.int32)
    page_dest_keys = jax.random.split(jax.random.fold_in(seeds[9], 1), (N_GROUP * N_TENSOR * PAGES_DEV) // PAGES_DEV)
    page_dest_turns = jax.random.permutation(jax.random.fold_in(seeds[9], 3), (N_GROUP * N_TENSOR * PAGES_DEV) // PAGES_DEV)
    page_dest = jax.vmap(lambda own, number: routed_block(jax.random.fold_in(seeds[9], 2), own, number, PAGES_DEV, N_GROUP, 1, CAP, 2))(page_dest_keys, page_dest_turns).reshape((N_GROUP * N_TENSOR * PAGES_DEV, 1))
    return {"hidden_in": hidden_in, "request_ids": request_ids, "norm_gains": norm_gains, "query_key_value_weight": query_key_value_weight, "w_out": w_out, "w_in": w_in, "w_down": w_down, "prefix_cache": prefix_cache, "prefix_owner": prefix_owner, "page_dest": page_dest}


ROPE_BASE = 100000.0
EPSILON = 1e-05
NEGATIVE_FILLER = -1e+30

def rms_norm(inputs, gain_row):
    floated = inputs.astype(jnp.float32)
    return floated * lax.rsqrt(lax.optimization_barrier(jnp.mean(floated * floated, axis=-1, keepdims=True)) + EPSILON) * gain_row

def apply_rotary(head_values, locate_position):
    half_dim = head_values.shape[-1] // 2
    frequency = ROPE_BASE ** (-jnp.arange(half_dim, dtype=jnp.float32) / half_dim)
    angles = locate_position.astype(jnp.float32)[:, None] * frequency[None, :]
    cosine = jnp.cos(angles)[:, None, :]
    sine_part = jnp.sin(angles)[:, None, :]
    first_half = head_values[..., :half_dim]
    second_half = head_values[..., half_dim:]
    return jnp.concatenate([first_half * cosine - second_half * sine_part, second_half * cosine + first_half * sine_part], axis=-1)

def positions(segment):
    row_number = segment.shape[0]
    row_index = jnp.arange(row_number, dtype=jnp.int32)
    same_request = segment[:, None] == segment[None, :]
    first_row = lax.optimization_barrier(jnp.min(jnp.where(same_request, row_index[None, :], row_number), axis=1)).astype(jnp.int32)
    return PREFIX_TOKENS + row_index - first_row

def layer_device(device_rows, segment, prefix_rows, norm_gains, query_key_value_weight, w_out, w_in, w_down):
    row_number = device_rows.shape[0]
    query_columns = QUERY_HEADS * HEAD_DIMENSION
    key_value_width = KEY_VALUE_HEADS * HEAD_DIMENSION
    normed = rms_norm(device_rows, norm_gains[0]).astype(jnp.bfloat16)
    projected_rows = jnp.dot(normed, query_key_value_weight, preferred_element_type=jnp.float32)
    locate_position = positions(segment)
    query_rows = apply_rotary(projected_rows[:, :query_columns].reshape(row_number, QUERY_HEADS, HEAD_DIMENSION), locate_position).astype(jnp.bfloat16)
    fresh_keys = apply_rotary(projected_rows[:, query_columns:query_columns + key_value_width].reshape(row_number, KEY_VALUE_HEADS, HEAD_DIMENSION), locate_position).astype(jnp.bfloat16)
    fresh_values = projected_rows[:, query_columns + key_value_width:].reshape(row_number, KEY_VALUE_HEADS, HEAD_DIMENSION).astype(jnp.bfloat16)
    joined_keys = jnp.concatenate([prefix_rows[:, :key_value_width].reshape(PREFIX_TOKENS, KEY_VALUE_HEADS, HEAD_DIMENSION), fresh_keys], axis=0)
    joined_values = jnp.concatenate([prefix_rows[:, key_value_width:].reshape(PREFIX_TOKENS, KEY_VALUE_HEADS, HEAD_DIMENSION), fresh_values], axis=0)
    query_groups = query_rows.reshape(row_number, KEY_VALUE_HEADS, QUERY_HEADS // KEY_VALUE_HEADS, HEAD_DIMENSION).astype(jnp.float32)
    scores = jnp.einsum('rkgd,nkd->rkgn', query_groups, joined_keys.astype(jnp.float32)) * HEAD_DIMENSION ** (-0.5)
    row_index = jnp.arange(row_number, dtype=jnp.int32)
    suffix_ok = (segment[None, :] == segment[:, None]) & (row_index[None, :] <= row_index[:, None])
    full_ok = jnp.concatenate([jnp.ones((row_number, PREFIX_TOKENS), dtype=bool), suffix_ok], axis=1)
    scores = jnp.where(full_ok[:, None, None, :], scores, NEGATIVE_FILLER)
    row_max = lax.optimization_barrier(jnp.max(scores, axis=-1, keepdims=True))
    weights = jnp.exp(scores - row_max)
    totals = lax.optimization_barrier(jnp.sum(weights, axis=-1))
    rounded = lax.optimization_barrier(weights.astype(jnp.bfloat16))
    summed = jnp.einsum('rkgn,nkd->rkgd', rounded.astype(jnp.float32), joined_values.astype(jnp.float32))
    attended = (summed / totals[..., None]).reshape(row_number, QUERY_HEADS * HEAD_DIMENSION).astype(jnp.bfloat16)
    middle = (device_rows.astype(jnp.float32) + jnp.dot(attended, w_out, preferred_element_type=jnp.float32)).astype(jnp.bfloat16)
    second = rms_norm(middle, norm_gains[1]).astype(jnp.bfloat16)
    gate_proj = jnp.dot(second, w_in[0], preferred_element_type=jnp.float32)
    up_proj = jnp.dot(second, w_in[1], preferred_element_type=jnp.float32)
    activated = (jax.nn.silu(gate_proj) * up_proj).astype(jnp.bfloat16)
    hidden_out = (middle.astype(jnp.float32) + jnp.dot(activated, w_down, preferred_element_type=jnp.float32)).astype(jnp.bfloat16)
    cache_rows = jnp.concatenate([fresh_keys.reshape(row_number, key_value_width), fresh_values.reshape(row_number, key_value_width)], axis=1)
    return (hidden_out, cache_rows)

def reference(hidden_in, request_ids, norm_gains, query_key_value_weight, w_out, w_in, w_down, prefix_cache, prefix_owner, page_dest):
    device_total = N_GROUP * N_TENSOR
    cache_columns = 2 * KEY_VALUE_HEADS * HEAD_DIMENSION
    blocked = prefix_cache.reshape(N_GROUP, N_TENSOR, PREFIX_TOKENS // N_TENSOR, cache_columns)
    prefix_rows = blocked[prefix_owner, jnp.arange(N_TENSOR, dtype=jnp.int32)].reshape(PREFIX_TOKENS, cache_columns)
    device_rows = hidden_in.reshape(device_total, TOK_DEV, MODEL_DIMENSION)

    def per_device(operand):
        return layer_device(operand[0], operand[1], prefix_rows, norm_gains, query_key_value_weight, w_out, w_in, w_down)
    outputs, caches = lax.map(per_device, (device_rows, request_ids))
    hidden_out = outputs.reshape(TOKENS, MODEL_DIMENSION)
    page_blocks = caches.reshape(N_GROUP, N_TENSOR, PAGES_DEV, PAGE * cache_columns).astype(jnp.float32)
    destination = page_dest.reshape(N_GROUP, N_TENSOR, PAGES_DEV)
    group_iota = jnp.arange(N_GROUP, dtype=jnp.int32)
    onehot = (destination[..., None] == group_iota).astype(jnp.int32)
    page_rank = lax.optimization_barrier(jnp.sum((jnp.cumsum(onehot, axis=2) - onehot) * onehot, axis=3))
    slot_iota = jnp.arange(CAP, dtype=jnp.int32)
    select = ((destination[..., None, None] == group_iota[:, None]) & (page_rank[..., None, None] == slot_iota[None, :])).astype(jnp.float32)
    placed = jnp.einsum('gtpdj,gtpc->dtgjc', select, page_blocks)
    suffix_cache = placed.reshape(N_GROUP, N_TENSOR, N_GROUP, CAP, PAGE, cache_columns).astype(jnp.bfloat16)
    return (hidden_out, suffix_cache)
```

```python
import jax
import jax.numpy as jnp
from jax import lax
from jax.sharding import PartitionSpec as P

QUERY_HEADS = 16
KEY_VALUE_HEADS = 8
HEAD_DIMENSION = 96
PREFIX_TOKENS = 1024
CAP = 8


ROPE_BASE = 100000.0
EPSILON = 1e-05
NEGATIVE_FILLER = -1e30


Z_SIZE = 4


def tensor_xor(value, tensor_count, z_bits):
    width = tensor_count // Z_SIZE
    pairs = [
        (z * width + y, (z ^ z_bits) * width + y) for z in range(Z_SIZE) for y in range(width)
    ]
    return lax.ppermute(value, "tensor", pairs)


def tensor_turn(value, tensor_count, step):
    width = tensor_count // Z_SIZE
    pairs = [
        (z * width + y, z * width + (y + step) % width)
        for z in range(Z_SIZE)
        for y in range(width)
    ]
    return lax.ppermute(value, "tensor", pairs)


def group_xor(value, group_count, bits):
    return lax.ppermute(value, "group", [(g, g ^ bits) for g in range(group_count)])


def gather_prefix(block, prefix_owner, group_count, tensor_count):
    group = lax.axis_index("group")
    owner = prefix_owner[lax.axis_index("tensor")]
    rows = block.shape[0] // group_count
    width = tensor_count // Z_SIZE
    quarter = lax.dynamic_slice_in_dim(block, group * rows, rows, 0)
    for bits in range(1, group_count):
        sent = lax.dynamic_slice_in_dim(block, (group ^ bits) * rows, rows, 0)
        came = group_xor(sent, group_count, bits)
        quarter = jnp.where(owner == (group ^ bits), came, quarter)
    line = jnp.concatenate(
        [quarter] + [tensor_xor(quarter, tensor_count, bits) for bits in range(1, Z_SIZE)]
    )
    plane = jnp.concatenate(
        [line] + [tensor_turn(line, tensor_count, step) for step in range(1, width)]
    )
    across = group_xor(plane, group_count, 2)
    own_rows = jnp.concatenate([plane, across])
    return [own_rows, group_xor(own_rows, group_count, 1)]


def gather_weights(w_in, w_down, group_count, tensor_count):
    group = lax.axis_index("group")
    across, core = group // 2, group % 2
    width = tensor_count // Z_SIZE
    part = w_in.shape[2] // 4

    def piece(side):
        start = (core * 2 + side) * part
        sliced = lax.dynamic_slice_in_dim(w_in, start, part, 2)
        return (
            jnp.concatenate([sliced[0], sliced[1]], axis=1),
            lax.dynamic_slice_in_dim(w_down, start, part, 0),
        )

    mine, other = piece(across), piece(1 - across)
    pieces = [mine, other]
    plane = [tuple(tensor_turn(v, tensor_count, step) for v in mine) for step in range(1, width)]
    far = tuple(tensor_xor(v, tensor_count, 2) for v in mine)
    pieces += plane
    pieces += [tuple(group_xor(v, group_count, 2) for v in got) for got in plane]
    far_across = tuple(group_xor(v, group_count, 2) for v in far)
    pieces += [far, far_across]
    for step in range(1, width):
        far_plane = tuple(tensor_turn(v, tensor_count, step) for v in far)
        pieces.append(far_plane)
        last = []
        for by_x, by_y in zip(far_plane, far_across):
            half = by_x.shape[0] // 2
            last.append(
                jnp.concatenate(
                    [
                        group_xor(by_x[:half], group_count, 2),
                        tensor_turn(by_y[half:], tensor_count, step),
                    ]
                )
            )
        pieces.append(tuple(last))
    return pieces


def rms_norm(inputs, gain_row):
    floated = inputs.astype(jnp.float32)
    return (
        floated
        * lax.rsqrt(jnp.mean(floated * floated, axis=-1, keepdims=True) + EPSILON)
        * gain_row
    )


def apply_rotary(head_values, locate_position):
    half_dim = head_values.shape[-1] // 2
    frequency = ROPE_BASE ** (-jnp.arange(half_dim, dtype=jnp.float32) / half_dim)
    angles = locate_position.astype(jnp.float32)[:, None] * frequency[None, :]
    cosine = jnp.cos(angles)[:, None, :]
    sine_part = jnp.sin(angles)[:, None, :]
    first_half = head_values[..., :half_dim]
    second_half = head_values[..., half_dim:]
    return jnp.concatenate(
        [
            first_half * cosine - second_half * sine_part,
            second_half * cosine + first_half * sine_part,
        ],
        axis=-1,
    )


def positions(segment):
    row_number = segment.shape[0]
    row_index = jnp.arange(row_number, dtype=jnp.int32)
    same_request = segment[:, None] == segment[None, :]
    first_row = jnp.min(jnp.where(same_request, row_index[None, :], row_number), axis=1)
    return PREFIX_TOKENS + row_index - first_row


def attend_update(attn_state, scores, value_head_rows):
    row_max, row_total, weighted = attn_state
    new_max = jnp.maximum(row_max, jnp.max(scores, axis=-1))
    weights = jnp.exp(scores - new_max[..., None])
    row_total = jnp.sum(weights, axis=-1)
    weighted = jnp.einsum(
        "rkgn,nkd->rkgd",
        weights.astype(jnp.bfloat16),
        value_head_rows,
        preferred_element_type=jnp.float32,
    )
    return (new_max, row_total, weighted)


def combine_states(left_state, right_state):
    new_max = jnp.maximum(left_state[0], right_state[0])
    left_factor = jnp.exp(left_state[0] - new_max)
    right_factor = jnp.exp(right_state[0] - new_max)
    row_total = left_state[1] * left_factor + right_state[1] * right_factor
    weighted = left_state[2] * left_factor[..., None] + right_state[2] * right_factor[..., None]
    return (new_max, row_total, weighted)


def expand_with(token_block, gate_and_up):
    both = jnp.dot(token_block, gate_and_up, preferred_element_type=jnp.float32)
    half = both.shape[1] // 2
    return (jax.nn.silu(both[:, :half]) * both[:, half:]).astype(jnp.bfloat16)


def feed_forward(second, pieces, group_count, tensor_count):
    beside = group_xor(second, group_count, 1)
    far = tensor_xor(second, tensor_count, 1)
    far_beside = group_xor(far, group_count, 1)
    down = jnp.concatenate([p[1] for p in pieces])

    def partial(left, right):
        tokens = jnp.concatenate([left, right])
        acts = jnp.concatenate([expand_with(tokens, p[0]) for p in pieces], axis=1)
        sums = jnp.dot(acts, down, preferred_element_type=jnp.float32)
        return sums[: left.shape[0]], sums[left.shape[0] :]

    far_sum, far_beside_sum = partial(far, far_beside)
    far_sum += group_xor(far_beside_sum.astype(jnp.bfloat16), group_count, 1).astype(jnp.float32)
    returned = tensor_xor(far_sum.astype(jnp.bfloat16), tensor_count, 1)
    own_sum, beside_sum = partial(second, beside)
    own_sum += group_xor(beside_sum.astype(jnp.bfloat16), group_count, 1).astype(jnp.float32)
    return own_sum + returned.astype(jnp.float32)


def on_device(
    hidden_in,
    request_ids,
    norm_gains,
    query_key_value_weight,
    w_out,
    w_in,
    w_down,
    prefix_cache,
    prefix_owner,
    page_dest,
):
    token_rows = hidden_in.shape[0]
    query_columns = QUERY_HEADS * HEAD_DIMENSION
    key_value_width = KEY_VALUE_HEADS * HEAD_DIMENSION
    group_count, tensor_count = lax.axis_size("group"), lax.axis_size("tensor")
    pieces = gather_weights(w_in, w_down, group_count, tensor_count)
    segment = request_ids[0]
    normed = rms_norm(hidden_in, norm_gains[0]).astype(jnp.bfloat16)
    projected_rows = jnp.dot(normed, query_key_value_weight, preferred_element_type=jnp.float32)
    locate_position = positions(segment)
    query_rows = apply_rotary(
        projected_rows[:, :query_columns].reshape(token_rows, QUERY_HEADS, HEAD_DIMENSION),
        locate_position,
    ).astype(jnp.bfloat16)
    fresh_keys = apply_rotary(
        projected_rows[:, query_columns : query_columns + key_value_width].reshape(
            token_rows, KEY_VALUE_HEADS, HEAD_DIMENSION
        ),
        locate_position,
    ).astype(jnp.bfloat16)
    fresh_values = (
        projected_rows[:, query_columns + key_value_width :]
        .reshape(token_rows, KEY_VALUE_HEADS, HEAD_DIMENSION)
        .astype(jnp.bfloat16)
    )
    query_groups = query_rows.reshape(
        token_rows, KEY_VALUE_HEADS, QUERY_HEADS // KEY_VALUE_HEADS, HEAD_DIMENSION
    )
    score_scale = HEAD_DIMENSION ** (-0.5)
    row_index = jnp.arange(token_rows, dtype=jnp.int32)
    allowed = (segment[None, :] == segment[:, None]) & (row_index[None, :] <= row_index[:, None])
    local_scores = (
        jnp.einsum("rkgd,nkd->rkgn", query_groups, fresh_keys, preferred_element_type=jnp.float32)
        * score_scale
    )
    local_scores = jnp.where(allowed[:, None, None, :], local_scores, NEGATIVE_FILLER)
    empty_state = (
        jnp.full(
            (token_rows, KEY_VALUE_HEADS, QUERY_HEADS // KEY_VALUE_HEADS),
            NEGATIVE_FILLER,
            jnp.float32,
        ),
        jnp.zeros((token_rows, KEY_VALUE_HEADS, QUERY_HEADS // KEY_VALUE_HEADS), jnp.float32),
        jnp.zeros(
            (token_rows, KEY_VALUE_HEADS, QUERY_HEADS // KEY_VALUE_HEADS, HEAD_DIMENSION),
            jnp.float32,
        ),
    )
    local_state = attend_update(empty_state, local_scores, fresh_values)
    loaded_pages = jnp.concatenate(
        gather_prefix(prefix_cache[0], prefix_owner, group_count, tensor_count)
    )
    key_total = loaded_pages.shape[0]
    key_head_rows = loaded_pages[:, :key_value_width].reshape(
        key_total, KEY_VALUE_HEADS, HEAD_DIMENSION
    )
    value_head_rows = loaded_pages[:, key_value_width:].reshape(
        key_total, KEY_VALUE_HEADS, HEAD_DIMENSION
    )
    scores = (
        jnp.einsum(
            "rkgd,nkd->rkgn", query_groups, key_head_rows, preferred_element_type=jnp.float32
        )
        * score_scale
    )
    attn_state = attend_update(empty_state, scores, value_head_rows)
    attn_state = combine_states(attn_state, local_state)
    attended = (
        (attn_state[2] / attn_state[1][..., None])
        .reshape(token_rows, QUERY_HEADS * HEAD_DIMENSION)
        .astype(jnp.bfloat16)
    )
    middle = (
        hidden_in.astype(jnp.float32) + jnp.dot(attended, w_out, preferred_element_type=jnp.float32)
    ).astype(jnp.bfloat16)
    second = rms_norm(middle, norm_gains[1]).astype(jnp.bfloat16)
    mlp_out = feed_forward(second, pieces, group_count, tensor_count)
    hidden_out = (middle.astype(jnp.float32) + mlp_out).astype(jnp.bfloat16)
    cache_rows = jnp.concatenate(
        [
            fresh_keys.reshape(token_rows, key_value_width),
            fresh_values.reshape(token_rows, key_value_width),
        ],
        axis=1,
    )
    page_count = page_dest.shape[0]
    page_blocks = cache_rows.reshape(page_count, token_rows // page_count, 2 * key_value_width)
    destination = page_dest[:, 0]
    dest_count = lax.axis_size("group")
    group_iota = jnp.arange(dest_count, dtype=jnp.int32)
    onehot = (destination[:, None] == group_iota[None, :]).astype(jnp.int32)
    page_rank = jnp.sum((jnp.cumsum(onehot, axis=0) - onehot) * onehot, axis=1)
    slot_iota = jnp.arange(CAP, dtype=jnp.int32)
    select = (
        (destination[:, None, None] == group_iota[None, :, None])
        & (page_rank[:, None, None] == slot_iota[None, None, :])
    ).astype(jnp.bfloat16)
    outgoing = jnp.einsum(
        "pdj,pxc->djxc", select, page_blocks, preferred_element_type=jnp.float32
    ).astype(jnp.bfloat16)
    received = lax.all_to_all(outgoing, "group", split_axis=0, concat_axis=0, tiled=True)
    return (hidden_out, received[None, None])


def solution(mesh):
    return jax.shard_map(
        on_device,
        mesh=mesh,
        in_specs=(
            P(("group", "tensor"), None),
            P(("group", "tensor"), None),
            P(),
            P(),
            P(),
            P(None, None, "tensor"),
            P("tensor", None),
            P("group", "tensor", None),
            P(),
            P(("group", "tensor"), None),
        ),
        out_specs=(P(("group", "tensor"), None), P("group", "tensor", None, None, None, None)),
        check_vma=False,
    )
```

```python
import functools

import jax
import jax.numpy as jnp
from jax import lax
from jax.experimental import pallas as pl
from jax.experimental.pallas import tpu as pltpu
from jax.sharding import PartitionSpec as P

QUERY_HEADS = 16
KEY_VALUE_HEADS = 8
HEAD_DIMENSION = 96
PREFIX_TOKENS = 1024
CAP = 8


ROPE_BASE = 100000.0
EPSILON = 1e-05
NEGATIVE_FILLER = -1e30
LOG2_E = 1.4426950408889634


Z_SIZE = 4


def tensor_xor(value, tensor_count, z_bits):
    width = tensor_count // Z_SIZE
    pairs = [
        (z * width + y, (z ^ z_bits) * width + y) for z in range(Z_SIZE) for y in range(width)
    ]
    return lax.ppermute(value, "tensor", pairs)


def tensor_turn(value, tensor_count, step):
    width = tensor_count // Z_SIZE
    pairs = [
        (z * width + y, z * width + (y + step) % width)
        for z in range(Z_SIZE)
        for y in range(width)
    ]
    return lax.ppermute(value, "tensor", pairs)


def group_xor(value, group_count, bits):
    return lax.ppermute(value, "group", [(g, g ^ bits) for g in range(group_count)])


def gather_prefix(block, prefix_owner, group_count, tensor_count):
    group = lax.axis_index("group")
    owner = prefix_owner[lax.axis_index("tensor")]
    rows = block.shape[0] // group_count
    width = tensor_count // Z_SIZE
    quarter = lax.dynamic_slice_in_dim(block, group * rows, rows, 0)
    for bits in range(1, group_count):
        sent = lax.dynamic_slice_in_dim(block, (group ^ bits) * rows, rows, 0)
        came = group_xor(sent, group_count, bits)
        quarter = jnp.where(owner == (group ^ bits), came, quarter)
    line = jnp.concatenate(
        [quarter] + [tensor_xor(quarter, tensor_count, bits) for bits in range(1, Z_SIZE)]
    )
    across = group_xor(line, group_count, 2)
    half = line.shape[0] // 2
    beside = [tensor_turn(line, tensor_count, step) for step in range(1, width)]
    corner = []
    for step in range(1, width):
        corner.append(group_xor(beside[step - 1][:half], group_count, 2))
        corner.append(tensor_turn(across[half:], tensor_count, step))
    pieces = [line, across] + beside + corner
    return pieces + [group_xor(piece, group_count, 1) for piece in pieces], quarter


def gather_weights(w_in, w_down, group_count, tensor_count):
    group = lax.axis_index("group")
    across, core = group // 2, group % 2
    width = tensor_count // Z_SIZE
    part = w_in.shape[2] // 4

    def piece(side):
        start = (core * 2 + side) * part
        sliced = lax.dynamic_slice_in_dim(w_in, start, part, 2)
        return (
            jnp.concatenate([sliced[0], sliced[1]], axis=1),
            lax.dynamic_slice_in_dim(w_down, start, part, 0),
        )

    mine, other = piece(across), piece(1 - across)
    pieces = [mine, other]
    plane = [tuple(tensor_turn(v, tensor_count, step) for v in mine) for step in range(1, width)]
    far = tuple(tensor_xor(v, tensor_count, 2) for v in mine)
    pieces += plane
    pieces += [tuple(group_xor(v, group_count, 2) for v in got) for got in plane]
    far_across = tuple(group_xor(v, group_count, 2) for v in far)
    pieces += [far, far_across]
    for step in range(1, width):
        far_plane = tuple(tensor_turn(v, tensor_count, step) for v in far)
        pieces.append(far_plane)
        last = []
        for by_x, by_y in zip(far_plane, far_across):
            half = by_x.shape[0] // 2
            last.append(
                jnp.concatenate(
                    [
                        group_xor(by_x[:half], group_count, 2),
                        tensor_turn(by_y[half:], tensor_count, step),
                    ]
                )
            )
        pieces.append(tuple(last))
    return pieces


def rms_norm(inputs, gain_row):
    floated = inputs.astype(jnp.float32)
    return (
        floated
        * lax.rsqrt(jnp.mean(floated * floated, axis=-1, keepdims=True) + EPSILON)
        * gain_row
    )


def positions(segment):
    row_number = segment.shape[0]
    row_index = jnp.arange(row_number, dtype=jnp.int32)
    same_request = segment[:, None] == segment[None, :]
    first_row = jnp.min(jnp.where(same_request, row_index[None, :], row_number), axis=1)
    return PREFIX_TOKENS + row_index - first_row


def rotary_tables(locate_position, width):
    half_dim = HEAD_DIMENSION // 2
    frequency = ROPE_BASE ** (-jnp.arange(half_dim, dtype=jnp.float32) / half_dim)
    angles = locate_position.astype(jnp.float32)[:, None] * frequency[None, :]
    cosine, sine = jnp.cos(angles), jnp.sin(angles)
    heads = width // HEAD_DIMENSION
    return jnp.tile(cosine, (1, 2 * heads)), jnp.tile(
        jnp.concatenate([-sine, sine], axis=1), (1, heads)
    )


def project_kernel(hidden, gain, weight, cosine, sine, *rest):
    out, normed = rest[-2:]
    step = pl.program_id(0)
    width = weight.shape[1]
    rotated_steps = (QUERY_HEADS + KEY_VALUE_HEADS) * HEAD_DIMENSION // width

    @pl.when(step == 0)
    def _():
        normed[...] = rms_norm(hidden[...], gain[...]).astype(jnp.bfloat16)

    projected = jnp.dot(normed[...], weight[...], preferred_element_type=jnp.float32)

    @pl.when(step < rotated_steps)
    def _():
        half_dim = HEAD_DIMENSION // 2
        lane = lax.broadcasted_iota(jnp.int32, projected.shape, 1)
        swapped = jnp.where(
            lane % HEAD_DIMENSION < half_dim,
            pltpu.roll(projected, width - half_dim, 1),
            pltpu.roll(projected, half_dim, 1),
        )
        out[...] = (projected * cosine[...] + swapped * sine[...]).astype(jnp.bfloat16)

    @pl.when(step >= rotated_steps)
    def _():
        out[...] = projected.astype(jnp.bfloat16)


def project(hidden_in, gain_row, weight, locate_position, earlier):
    rows, depth = hidden_in.shape
    columns = weight.shape[1]
    width = 4 * HEAD_DIMENSION
    cosine, sine = rotary_tables(locate_position, width)
    whole = lambda shape: pl.BlockSpec(shape, lambda i: (0, 0))
    return pl.pallas_call(
        project_kernel,
        grid=(columns // width,),
        in_specs=[
            whole((rows, depth)),
            whole((1, depth)),
            pl.BlockSpec((depth, width), lambda i: (0, i)),
            whole((rows, width)),
            whole((rows, width)),
        ]
        + [pl.BlockSpec(memory_space=pl.ANY)] * len(earlier),
        out_specs=pl.BlockSpec((rows, width), lambda i: (0, i)),
        out_shape=jax.ShapeDtypeStruct((rows, columns), jnp.bfloat16),
        scratch_shapes=[pltpu.VMEM((rows, depth), jnp.bfloat16)],
        compiler_params=pltpu.CompilerParams(vmem_limit_bytes=24 << 20),
        cost_estimate=pl.CostEstimate(
            flops=2 * rows * depth * columns,
            bytes_accessed=2 * depth * columns,
            transcendentals=0,
        ),
    )(hidden_in, gain_row[None, :], weight, cosine, sine, *earlier)


def attention_kernel(piece_count, row_ids, column_ids, projected, *rest):
    pieces, out, joined = rest[:piece_count], rest[-2], rest[-1]
    rows = projected.shape[0]
    query_columns = QUERY_HEADS * HEAD_DIMENSION
    key_value_width = KEY_VALUE_HEADS * HEAD_DIMENSION
    repeats = QUERY_HEADS // KEY_VALUE_HEADS
    at = 0
    for piece in pieces:
        joined[at : at + piece.shape[0], :] = piece[...]
        at += piece.shape[0]
    joined[at : at + rows, :] = projected[:, query_columns:]
    row_index = lax.broadcasted_iota(jnp.int32, (rows, rows), 0)
    column_index = lax.broadcasted_iota(jnp.int32, (rows, rows), 1)
    allowed = (row_ids[...] == column_ids[...]) & (column_index <= row_index)
    allowed = jnp.concatenate([allowed] * repeats, axis=0)
    scale = HEAD_DIMENSION ** (-0.5) * LOG2_E

    def head_columns(index):
        return slice(index * HEAD_DIMENSION, (index + 1) * HEAD_DIMENSION)

    for head in range(KEY_VALUE_HEADS):
        queries = jnp.concatenate(
            [projected[:, head_columns(head * repeats + g)] for g in range(repeats)], axis=0
        )
        keys = joined[:, head_columns(head)]
        values = joined[:, head_columns(KEY_VALUE_HEADS + head)]
        scores = lax.dot_general(
            queries, keys, (((1,), (1,)), ((), ())), preferred_element_type=jnp.float32
        )
        scores = jnp.concatenate(
            [scores[:, :at], jnp.where(allowed, scores[:, at:], NEGATIVE_FILLER)], axis=1
        )
        top = jnp.max(scores, axis=1, keepdims=True)
        weights = jnp.exp2((scores - top) * scale)
        total = jnp.sum(weights, axis=1, keepdims=True)
        summed = jnp.dot(
            weights.astype(jnp.bfloat16), values, preferred_element_type=jnp.float32
        )
        attended = (summed / total).astype(jnp.bfloat16)
        for g in range(repeats):
            out[:, head_columns(head * repeats + g)] = attended[g * rows : (g + 1) * rows]


def attend(segment, projected, pieces, earlier):
    rows = projected.shape[0]
    columns = QUERY_HEADS * HEAD_DIMENSION
    key_count = rows + sum(piece.shape[0] for piece in pieces)
    vmem = pl.BlockSpec(memory_space=pltpu.VMEM)
    return pl.pallas_call(
        functools.partial(attention_kernel, len(pieces)),
        in_specs=[vmem] * (3 + len(pieces)) + [pl.BlockSpec(memory_space=pl.ANY)] * len(earlier),
        out_specs=vmem,
        out_shape=jax.ShapeDtypeStruct((rows, columns), jnp.bfloat16),
        scratch_shapes=[pltpu.VMEM((key_count, pieces[0].shape[1]), jnp.bfloat16)],
        compiler_params=pltpu.CompilerParams(vmem_limit_bytes=40 << 20),
        cost_estimate=pl.CostEstimate(
            flops=4 * rows * key_count * columns,
            bytes_accessed=2 * key_count * columns,
            transcendentals=rows * QUERY_HEADS * key_count,
        ),
    )(segment[:, None], segment[None, :], projected, *pieces, *earlier)


def expand_with(token_block, gate_and_up):
    both = jnp.dot(token_block, gate_and_up, preferred_element_type=jnp.float32)
    half = both.shape[1] // 2
    return (jax.nn.silu(both[:, :half]) * both[:, half:]).astype(jnp.bfloat16)


def feed_forward(second, pieces, group_count, tensor_count):
    beside = group_xor(second, group_count, 1)
    far = tensor_xor(second, tensor_count, 1)
    far_beside = group_xor(far, group_count, 1)
    down = jnp.concatenate([p[1] for p in pieces])

    def partial(left, right):
        tokens = jnp.concatenate([left, right])
        acts = jnp.concatenate([expand_with(tokens, p[0]) for p in pieces], axis=1)
        sums = jnp.dot(acts, down, preferred_element_type=jnp.float32)
        return sums[: left.shape[0]], sums[left.shape[0] :]

    far_sum, far_beside_sum = partial(far, far_beside)
    far_sum += group_xor(far_beside_sum.astype(jnp.bfloat16), group_count, 1).astype(jnp.float32)
    returned = tensor_xor(far_sum.astype(jnp.bfloat16), tensor_count, 1)
    own_sum, beside_sum = partial(second, beside)
    own_sum += group_xor(beside_sum.astype(jnp.bfloat16), group_count, 1).astype(jnp.float32)
    return own_sum + returned.astype(jnp.float32)


def on_device(
    hidden_in,
    request_ids,
    norm_gains,
    query_key_value_weight,
    w_out,
    w_in,
    w_down,
    prefix_cache,
    prefix_owner,
    page_dest,
):
    token_rows = hidden_in.shape[0]
    query_columns = QUERY_HEADS * HEAD_DIMENSION
    group_count, tensor_count = lax.axis_size("group"), lax.axis_size("tensor")
    pieces = gather_weights(w_in, w_down, group_count, tensor_count)
    segment = request_ids[0]
    prefix_pieces, quarter = gather_prefix(
        prefix_cache[0], prefix_owner, group_count, tensor_count
    )
    projected = project(
        hidden_in, norm_gains[0], query_key_value_weight, positions(segment), [quarter]
    )
    attended = attend(segment, projected, prefix_pieces, [])
    middle = (
        hidden_in.astype(jnp.float32) + jnp.dot(attended, w_out, preferred_element_type=jnp.float32)
    ).astype(jnp.bfloat16)
    second = rms_norm(middle, norm_gains[1]).astype(jnp.bfloat16)
    mlp_out = feed_forward(second, pieces, group_count, tensor_count)
    hidden_out = (middle.astype(jnp.float32) + mlp_out).astype(jnp.bfloat16)
    cache_rows = projected[:, query_columns:]
    page_count = page_dest.shape[0]
    page_blocks = cache_rows.reshape(
        page_count, token_rows // page_count, cache_rows.shape[1]
    )
    destination = page_dest[:, 0]
    dest_count = lax.axis_size("group")
    group_iota = jnp.arange(dest_count, dtype=jnp.int32)
    onehot = (destination[:, None] == group_iota[None, :]).astype(jnp.int32)
    page_rank = jnp.sum((jnp.cumsum(onehot, axis=0) - onehot) * onehot, axis=1)
    slot_iota = jnp.arange(CAP, dtype=jnp.int32)
    select = (
        (destination[:, None, None] == group_iota[None, :, None])
        & (page_rank[:, None, None] == slot_iota[None, None, :])
    ).astype(jnp.bfloat16)
    outgoing = jnp.einsum(
        "pdj,pxc->djxc", select, page_blocks, preferred_element_type=jnp.float32
    ).astype(jnp.bfloat16)
    received = lax.all_to_all(outgoing, "group", split_axis=0, concat_axis=0, tiled=True)
    return (hidden_out, received[None, None])


def solution(mesh):
    return jax.shard_map(
        on_device,
        mesh=mesh,
        in_specs=(
            P(("group", "tensor"), None),
            P(("group", "tensor"), None),
            P(),
            P(),
            P(),
            P(None, None, "tensor"),
            P("tensor", None),
            P("group", "tensor", None),
            P(),
            P(("group", "tensor"), None),
        ),
        out_specs=(P(("group", "tensor"), None), P("group", "tensor", None, None, None, None)),
        check_vma=False,
    )
```

```python
import functools

import jax
import jax.numpy as jnp
from jax import lax
from jax.experimental import pallas as pl
from jax.experimental.pallas import tpu as pltpu
from jax.sharding import PartitionSpec as P

QUERY_HEADS = 16
KEY_VALUE_HEADS = 8
HEAD_DIMENSION = 96
PREFIX_TOKENS = 1024
CAP = 8


ROPE_BASE = 100000.0
EPSILON = 1e-05
NEGATIVE_FILLER = -1e30
LOG2_E = 1.4426950408889634


Z_SIZE = 4


def tensor_xor(value, tensor_count, z_bits):
    width = tensor_count // Z_SIZE
    pairs = [
        (z * width + y, (z ^ z_bits) * width + y) for z in range(Z_SIZE) for y in range(width)
    ]
    return lax.ppermute(value, "tensor", pairs)


def tensor_turn(value, tensor_count, step):
    width = tensor_count // Z_SIZE
    pairs = [
        (z * width + y, z * width + (y + step) % width)
        for z in range(Z_SIZE)
        for y in range(width)
    ]
    return lax.ppermute(value, "tensor", pairs)


def group_xor(value, group_count, bits):
    return lax.ppermute(value, "group", [(g, g ^ bits) for g in range(group_count)])


def own_quarter(block, prefix_owner, group_count):
    group = lax.axis_index("group")
    owner = prefix_owner[lax.axis_index("tensor")]
    rows = block.shape[0] // group_count
    quarter = block[:rows]
    for bits in range(1, group_count):
        came = group_xor(block[bits * rows : (bits + 1) * rows], group_count, bits)
        quarter = jnp.where(owner == (group ^ bits), came, quarter)
    return quarter


HBM = pl.BlockSpec(memory_space=pltpu.HBM)
ANYWHERE = pl.BlockSpec(memory_space=pl.ANY)


def whole(array):
    return pl.BlockSpec(array.shape, lambda *_: (0,) * len(array.shape))


def wholes(arrays):
    return [whole(array) for array in arrays]


def after(value, *earlier):
    return lax.optimization_barrier((value, *earlier))[0]


def swap_in_plane(value, x_core, group_count, tensor_count):
    pairs = []
    for group in range(group_count):
        for place in range(tensor_count):
            over_x = group % 2 == x_core
            target = (group ^ 2, place) if over_x else (group, place ^ 1)
            pairs.append((group * tensor_count + place, target[0] * tensor_count + target[1]))
    return lax.ppermute(value, ("group", "tensor"), pairs)


def plane_pair(value, group_count, tensor_count):
    if tensor_count != 2 * Z_SIZE:
        return [value, group_xor(value, group_count, 2)]
    return [value, swap_in_plane(value, 0, group_count, tensor_count)]


def plane_rest(pair, group_count, tensor_count):
    width = tensor_count // Z_SIZE
    if width != 2:
        return [tensor_turn(v, tensor_count, step) for step in range(1, width) for v in pair]
    return [swap_in_plane(v, 1, group_count, tensor_count) for v in pair]


def pack_kernel(side, w_in, w_down, inward, down):
    part = w_in.shape[2] // 2
    columns = pl.ds(pl.multiple_of(side[0] * part, part), part)
    for half in range(2):
        inward[:, half * part : (half + 1) * part] = w_in[half, :, columns]
    for block in range(down.shape[0] // part):
        down[block * part : (block + 1) * part, :] = w_down[
            columns, block * 2 * part : (block + 1) * 2 * part
        ]


def join_piece(gate, up, down):
    width = 2 * gate.shape[1]
    blocks = [down[:, at : at + width] for at in range(0, down.shape[1], width)]
    return jnp.concatenate([gate, up], axis=1), jnp.concatenate(blocks)


def split_piece(piece):
    inward, down = piece
    part = inward.shape[1] // 2
    blocks = [down[at : at + part] for at in range(0, down.shape[0], part)]
    return inward[:, :part], inward[:, part:], jnp.concatenate(blocks, axis=1)


def own_piece(w_in, w_down, side):
    core = lax.axis_index("group") % 2
    depth, part = w_in.shape[1], w_in.shape[2] // 4
    if part % 128:
        start = (core * 2 + side) * part
        return join_piece(
            lax.dynamic_slice_in_dim(w_in[0], start, part, 1),
            lax.dynamic_slice_in_dim(w_in[1], start, part, 1),
            lax.dynamic_slice_in_dim(w_down, start, part, 0),
        )
    steps = depth // (4 * part)
    shapes = [(depth, 2 * part), (depth // 2, 2 * part)]
    return pl.pallas_call(
        pack_kernel,
        grid_spec=pltpu.PrefetchScalarGridSpec(
            num_scalar_prefetch=1,
            grid=(steps,),
            in_specs=[
                pl.BlockSpec((2, depth // steps, 2 * part), lambda i, at: (0, i, at[1])),
                pl.BlockSpec((2 * part, depth // steps), lambda i, at: (at[1], i)),
            ],
            out_specs=[
                pl.BlockSpec((rows // steps, columns), lambda i, at: (i, 0))
                for rows, columns in shapes
            ],
        ),
        out_shape=[jax.ShapeDtypeStruct(shape, w_in.dtype) for shape in shapes],
        compiler_params=pltpu.CompilerParams(vmem_limit_bytes=60 << 20),
    )(jnp.stack([side, core]).astype(jnp.int32), w_in, w_down)


def merge_pieces(pieces):
    count = max(1, 128 // (pieces[0][0].shape[1] // 2))
    if count == 1:
        return pieces
    merged = []
    for at in range(0, len(pieces), count):
        gates, ups, downs = zip(*[split_piece(p) for p in pieces[at : at + count]])
        merged.append(
            join_piece(
                jnp.concatenate(gates, axis=1),
                jnp.concatenate(ups, axis=1),
                jnp.concatenate(downs),
            )
        )
    return merged


def rms_norm(inputs, gain_row):
    floated = inputs.astype(jnp.float32)
    return (
        floated
        * lax.rsqrt(jnp.mean(floated * floated, axis=-1, keepdims=True) + EPSILON)
        * gain_row
    )


def positions(segment):
    row_number = segment.shape[0]
    row_index = jnp.arange(row_number, dtype=jnp.int32)
    same_request = segment[:, None] == segment[None, :]
    first_row = jnp.min(jnp.where(same_request, row_index[None, :], row_number), axis=1)
    return PREFIX_TOKENS + row_index - first_row


def rotary_tables(locate_position, width):
    half_dim = HEAD_DIMENSION // 2
    frequency = ROPE_BASE ** (-jnp.arange(half_dim, dtype=jnp.float32) / half_dim)
    angles = locate_position.astype(jnp.float32)[:, None] * frequency[None, :]
    cosine, sine = jnp.cos(angles), jnp.sin(angles)
    heads = width // HEAD_DIMENSION
    return jnp.tile(cosine, (1, 2 * heads)), jnp.tile(
        jnp.concatenate([-sine, sine], axis=1), (1, heads)
    )


def project_kernel(hidden, gain, weight, cosine, sine, *rest):
    out, normed = rest[-2:]
    step = pl.program_id(0)
    width = weight.shape[1]
    rotated_steps = (QUERY_HEADS + KEY_VALUE_HEADS) * HEAD_DIMENSION // width

    @pl.when(step == 0)
    def _():
        normed[...] = rms_norm(hidden[...], gain[...]).astype(jnp.bfloat16)

    projected = jnp.dot(normed[...], weight[...], preferred_element_type=jnp.float32)

    @pl.when(step < rotated_steps)
    def _():
        half_dim = HEAD_DIMENSION // 2
        lane = lax.broadcasted_iota(jnp.int32, projected.shape, 1)
        swapped = jnp.where(
            lane % HEAD_DIMENSION < half_dim,
            pltpu.roll(projected, width - half_dim, 1),
            pltpu.roll(projected, half_dim, 1),
        )
        heads = width // HEAD_DIMENSION
        cosines = jnp.concatenate([cosine[...]] * heads, axis=1)
        sines = jnp.concatenate([sine[...]] * heads, axis=1)
        out[...] = (projected * cosines + swapped * sines).astype(jnp.bfloat16)

    @pl.when(step >= rotated_steps)
    def _():
        out[...] = projected.astype(jnp.bfloat16)


def project(hidden_in, gain_row, weight, locate_position, earlier):
    rows, depth = hidden_in.shape
    columns = weight.shape[1]
    width = 8 * HEAD_DIMENSION
    cosine, sine = rotary_tables(locate_position, HEAD_DIMENSION)
    return pl.pallas_call(
        project_kernel,
        grid=(columns // width,),
        in_specs=[
            whole(hidden_in),
            whole(gain_row[None, :]),
            pl.BlockSpec((depth, width), lambda i: (0, i)),
            whole(cosine),
            whole(sine),
        ]
        + [pl.BlockSpec(memory_space=pl.ANY)] * len(earlier),
        out_specs=pl.BlockSpec((rows, width), lambda i: (0, i)),
        out_shape=jax.ShapeDtypeStruct((rows, columns), jnp.bfloat16),
        scratch_shapes=[pltpu.VMEM((rows, depth), jnp.bfloat16)],
        compiler_params=pltpu.CompilerParams(vmem_limit_bytes=60 << 20),
        cost_estimate=pl.CostEstimate(
            flops=2 * rows * depth * columns,
            bytes_accessed=2 * depth * columns,
            transcendentals=0,
        ),
    )(hidden_in, gain_row[None, :], weight, cosine, sine, *earlier)


def head_columns(index):
    return slice(index * HEAD_DIMENSION, (index + 1) * HEAD_DIMENSION)


def attention_kernel(piece_count, heads, row_ids, column_ids, projected, *rest):
    pieces, out, joined, semaphores = rest[:piece_count], *rest[-3:]
    rows = projected.shape[0]
    repeats = QUERY_HEADS // KEY_VALUE_HEADS
    first, count = heads
    width = count * HEAD_DIMENSION
    key_value_width = KEY_VALUE_HEADS * HEAD_DIMENSION
    copies, at = [], 0
    for index, piece in enumerate(pieces):
        for side in range(2):
            start = side * key_value_width + first * HEAD_DIMENSION
            source = piece.at[:, pl.ds(start, width)]
            target = joined.at[pl.ds(at, piece.shape[0]), pl.ds(side * width, width)]
            copies.append(pltpu.make_async_copy(source, target, semaphores.at[2 * index + side]))
        at += piece.shape[0]
    for copy in copies:
        copy.start()
    for side in range(2):
        start = (QUERY_HEADS + side * KEY_VALUE_HEADS + first) * HEAD_DIMENSION
        joined[at : at + rows, side * width : (side + 1) * width] = projected[
            :, start : start + width
        ]
    row_index = lax.broadcasted_iota(jnp.int32, (rows, rows), 0)
    column_index = lax.broadcasted_iota(jnp.int32, (rows, rows), 1)
    allowed = (row_ids[...] == column_ids[...]) & (column_index <= row_index)
    allowed = jnp.concatenate([allowed] * repeats, axis=0)
    scale = HEAD_DIMENSION ** (-0.5) * LOG2_E
    for copy in copies:
        copy.wait()
    for head in range(count):
        queries = jnp.concatenate(
            [projected[:, head_columns((first + head) * repeats + g)] for g in range(repeats)],
            axis=0,
        )
        scores = lax.dot_general(
            queries,
            joined[:, head_columns(head)],
            (((1,), (1,)), ((), ())),
            preferred_element_type=jnp.float32,
        )
        scores = jnp.concatenate(
            [scores[:, :at], jnp.where(allowed, scores[:, at:], NEGATIVE_FILLER)], axis=1
        )
        top = jnp.max(scores, axis=1, keepdims=True)
        weights = jnp.exp2((scores - top) * scale)
        total = jnp.sum(weights, axis=1, keepdims=True)
        summed = jnp.dot(
            weights.astype(jnp.bfloat16),
            joined[:, head_columns(count + head)],
            preferred_element_type=jnp.float32,
        )
        attended = (summed / total).astype(jnp.bfloat16)
        for g in range(repeats):
            out[:, head_columns(head * repeats + g)] = attended[g * rows : (g + 1) * rows]


def last_attention_kernel(
    piece_count, heads, row_ids, column_ids, projected, hidden, gain, *rest
):
    pieces, w_out = rest[:piece_count], rest[piece_count]
    middle, second, joined, semaphores, out, weight, semaphore = rest[-7:]
    fetch = pltpu.make_async_copy(w_out, weight, semaphore)
    fetch.start()
    attention_kernel(
        piece_count, heads, row_ids, column_ids, projected, *pieces, out, joined, semaphores
    )
    fetch.wait()
    added = jnp.dot(out[...], weight[...], preferred_element_type=jnp.float32)
    middle[...] = (hidden[...].astype(jnp.float32) + added).astype(jnp.bfloat16)
    second[...] = rms_norm(middle[...], gain[...]).astype(jnp.bfloat16)


def attend(segment, projected, pieces, heads, rest=None):
    rows = projected.shape[0]
    key_count = rows + sum(piece.shape[0] for piece in pieces)
    width = heads[1] * HEAD_DIMENSION
    columns = width * QUERY_HEADS // KEY_VALUE_HEADS
    resident = [segment[:, None], segment[None, :], projected]
    remote = list(pieces)
    kernel = attention_kernel
    out = [jax.ShapeDtypeStruct((rows, columns), jnp.bfloat16)]
    scratch = [
        pltpu.VMEM((key_count, 2 * width), jnp.bfloat16),
        pltpu.SemaphoreType.DMA((2 * len(pieces),)),
    ]
    if rest is not None:
        hidden_in, gain_row, w_out = rest
        resident += [hidden_in, gain_row[None, :]]
        remote.append(w_out)
        kernel = last_attention_kernel
        out = [jax.ShapeDtypeStruct(hidden_in.shape, jnp.bfloat16)] * 2
        scratch += [
            pltpu.VMEM((rows, columns), jnp.bfloat16),
            pltpu.VMEM(w_out.shape, jnp.bfloat16),
            pltpu.SemaphoreType.DMA,
        ]
    return pl.pallas_call(
        functools.partial(kernel, len(pieces), heads),
        grid=(1,),
        in_specs=wholes(resident) + [HBM] * len(remote),
        out_specs=wholes(out),
        out_shape=out,
        scratch_shapes=scratch,
        compiler_params=pltpu.CompilerParams(vmem_limit_bytes=60 << 20),
    )(*resident, *remote)


def feed_forward_kernel(piece_count, carry_count, left, right, *rest):
    weights = rest[: 2 * piece_count]
    carries = rest[2 * piece_count : 2 * piece_count + carry_count]
    left_out, right_out, tokens, acts = rest[-4:]
    rows, depth = left.shape
    part = weights[0].shape[1] // 2
    tokens[:rows, :] = left[...]
    tokens[rows:, :] = right[...]
    for index in range(piece_count):
        both = jnp.dot(tokens[...], weights[2 * index][...], preferred_element_type=jnp.float32)
        gate, up = both[:, :part], both[:, part:]
        acts[:, index * part : (index + 1) * part] = (gate / (1.0 + jnp.exp(-gate)) * up).astype(
            jnp.bfloat16
        )
    for block in range(depth // (2 * part)):
        columns = slice(block * 2 * part, (block + 1) * 2 * part)
        weight = jnp.concatenate(
            [v[block * part : (block + 1) * part, :] for v in weights[1::2]]
        )
        sums = jnp.dot(acts[...], weight, preferred_element_type=jnp.float32)
        for side, out in enumerate((left_out, right_out)):
            found = sums[side * rows : (side + 1) * rows]
            for carry in carries[side::2]:
                found += carry[:, columns].astype(jnp.float32)
            out[:, columns] = found.astype(out.dtype)


def feed_forward(left, right, pieces, carries, right_dtype, earlier=()):
    rows, depth = left.shape
    part = pieces[0][0].shape[1] // 2
    chunks = [chunk for piece in pieces for chunk in piece]
    out = [jax.ShapeDtypeStruct((rows, depth), dtype) for dtype in (jnp.float32, right_dtype)]
    return pl.pallas_call(
        functools.partial(feed_forward_kernel, len(pieces), len(carries)),
        grid=(1,),
        in_specs=wholes([left, right, *chunks, *carries]) + [ANYWHERE] * len(earlier),
        out_specs=wholes(out),
        out_shape=out,
        scratch_shapes=[
            pltpu.VMEM((2 * rows, depth), jnp.bfloat16),
            pltpu.VMEM((2 * rows, part * len(pieces)), jnp.bfloat16),
        ],
        compiler_params=pltpu.CompilerParams(vmem_limit_bytes=32 << 20),
    )(left, right, *chunks, *carries, *earlier)


def add_rows(first, *others):
    def kernel(*refs):
        refs[-1][...] = sum(ref[...].astype(jnp.float32) for ref in refs[:-1]).astype(jnp.bfloat16)

    return pl.pallas_call(
        kernel,
        grid=(1,),
        in_specs=wholes([first, *others]),
        out_specs=whole(first),
        out_shape=jax.ShapeDtypeStruct(first.shape, jnp.bfloat16),
    )(first, *others)


def select_kernel(group_count, table, projected, *rest):
    outs = rest[-group_count:]
    page_rows = outs[0].shape[0] // CAP
    columns = outs[0].shape[1]
    for index in range(group_count * CAP):
        page = table[index]
        start = pl.multiple_of(jnp.maximum(page, 0) * page_rows, page_rows)
        rows = projected[pl.ds(start, page_rows), columns:]
        slot = index % CAP
        outs[index // CAP][slot * page_rows : (slot + 1) * page_rows, :] = jnp.where(
            page >= 0, rows, jnp.zeros_like(rows)
        )


def select_pages(projected, destination, group_count, earlier):
    page_count = destination.shape[0]
    page_rows = projected.shape[0] // page_count
    group = lax.axis_index("group")
    same = destination[:, None] == destination[None, :]
    page = jnp.arange(page_count, dtype=jnp.int32)
    rank = jnp.sum(same & (page[None, :] < page[:, None]), axis=1, dtype=jnp.int32)
    slot = (destination ^ group) * CAP + rank
    chosen = slot[None, :] == jnp.arange(group_count * CAP, dtype=jnp.int32)[:, None]
    table = jnp.max(jnp.where(chosen, page[None, :], -1), axis=1)
    columns = projected.shape[1] // 2
    out = [jax.ShapeDtypeStruct((CAP * page_rows, columns), projected.dtype)] * group_count
    return pl.pallas_call(
        functools.partial(select_kernel, group_count),
        grid_spec=pltpu.PrefetchScalarGridSpec(
            num_scalar_prefetch=1,
            grid=(1,),
            in_specs=[whole(projected)] + [ANYWHERE] * len(earlier),
            out_specs=wholes(out),
        ),
        out_shape=out,
        compiler_params=pltpu.CompilerParams(vmem_limit_bytes=16 << 20),
    )(table, projected, *earlier)


def place_kernel(group, *rest):
    *received, out = rest
    for bits, block in enumerate(received):
        out[group[0] ^ bits] = block[...]


def place_pages(received):
    out = jax.ShapeDtypeStruct((len(received), *received[0].shape), received[0].dtype)
    return pl.pallas_call(
        place_kernel,
        grid_spec=pltpu.PrefetchScalarGridSpec(
            num_scalar_prefetch=1,
            grid=(1,),
            in_specs=wholes(received),
            out_specs=whole(out),
        ),
        out_shape=out,
    )(lax.axis_index("group")[None].astype(jnp.int32), *received)


def on_device(
    hidden_in,
    request_ids,
    norm_gains,
    query_key_value_weight,
    w_out,
    w_in,
    w_down,
    prefix_cache,
    prefix_owner,
    page_dest,
):
    group_count, tensor_count = lax.axis_size("group"), lax.axis_size("tensor")
    sizes = (group_count, tensor_count)
    turns = range(1, tensor_count // Z_SIZE)
    segment = request_ids[0]
    quarter = own_quarter(prefix_cache[0], prefix_owner, group_count)
    across = lax.axis_index("group") // 2
    mine = own_piece(w_in, w_down, across)
    far_down = tensor_xor(mine[1], tensor_count, 2)
    inward = [tensor_turn(mine[0], tensor_count, step) for step in turns]
    along_z = [tensor_xor(quarter, tensor_count, bits) for bits in range(1, Z_SIZE)]
    projected = project(
        after(hidden_in, mine[0], quarter),
        norm_gains[0],
        query_key_value_weight,
        positions(segment),
        [],
    )
    line = after(jnp.concatenate([quarter] + along_z), projected, far_down)
    other = own_piece(w_in, w_down, after(1 - across, projected))
    far_in = tensor_xor(after(mine[0], line), tensor_count, 2)
    lines = plane_pair(line, *sizes)
    lines = after(jnp.concatenate(lines), inward[0])
    across = [group_xor(after(v, lines), group_count, 2) for v in inward]
    lines = [lines] + plane_rest([lines], *sizes)
    down_pair = plane_pair(far_down, *sizes)
    down = [[tensor_turn(v, tensor_count, step) for v in (mine[1], other[1])] for step in turns]
    near = []
    for step in range(len(turns)):
        near += [(inward[step], down[step][0]), (across[step], down[step][1])]
    lines += [group_xor(v, group_count, 1) for v in lines]
    middle, second = attend(
        segment,
        projected,
        lines,
        (0, KEY_VALUE_HEADS),
        (hidden_in, norm_gains[1], w_out),
    )
    far = after(second, far_in, across[0], *down[0], down_pair[1])
    far = tensor_xor(far, tensor_count, 1)
    in_pair = plane_pair(far_in, *sizes)
    late = [pair + plane_rest(pair, *sizes) for pair in (in_pair, down_pair)]
    late = list(zip(*late))
    beside = group_xor(second, group_count, 1)
    far_beside = group_xor(far, group_count, 1)
    near = merge_pieces([mine, other] + near)
    late = merge_pieces(late)
    own_early = feed_forward(second, beside, near, [], jnp.float32)
    far_early = feed_forward(far, far_beside, near, [], jnp.float32, own_early)
    outgoing = select_pages(projected, page_dest[:, 0], group_count, [far])
    far_sum, far_beside_sum = feed_forward(
        far, far_beside, late, far_early, jnp.bfloat16, [outgoing[0]]
    )
    far_sum = far_sum + group_xor(far_beside_sum, group_count, 1).astype(jnp.float32)
    far_sum = far_sum.astype(jnp.bfloat16)
    returned = tensor_xor(far_sum, tensor_count, 1)
    received = [outgoing[0]] + [
        group_xor(outgoing[bits], group_count, bits) for bits in range(1, group_count)
    ]
    own_sum, beside_sum = feed_forward(
        after(second, far_sum, *received[1:]), beside, late, [*own_early, middle], jnp.bfloat16
    )
    own_beside = group_xor(beside_sum, group_count, 1)
    received = place_pages(received)
    hidden_out = add_rows(own_sum, own_beside, after(returned, received))
    pages = received.reshape(group_count, CAP, -1, received.shape[2])
    return (hidden_out, pages[None, None])


def solution(mesh):
    return jax.shard_map(
        on_device,
        mesh=mesh,
        in_specs=(
            P(("group", "tensor"), None),
            P(("group", "tensor"), None),
            P(),
            P(),
            P(),
            P(None, None, "tensor"),
            P("tensor", None),
            P("group", "tensor", None),
            P(),
            P(("group", "tensor"), None),
        ),
        out_specs=(P(("group", "tensor"), None), P("group", "tensor", None, None, None, None)),
        check_vma=False,
    )
```

```python
import functools

import jax
import jax.numpy as jnp
from jax import lax
from jax.experimental import pallas as pl
from jax.experimental.pallas import tpu as pltpu
from jax.sharding import PartitionSpec as P

QUERY_HEADS = 16
KEY_VALUE_HEADS = 8
HEAD_DIMENSION = 96
PREFIX_TOKENS = 1024
CAP = 8


ROPE_BASE = 100000.0
EPSILON = 1e-05
NEGATIVE_FILLER = -1e30
LOG2_E = 1.4426950408889634


Z_SIZE = 4


def tensor_xor(value, tensor_count, z_bits):
    width = tensor_count // Z_SIZE
    pairs = [
        (z * width + y, (z ^ z_bits) * width + y) for z in range(Z_SIZE) for y in range(width)
    ]
    return lax.ppermute(value, "tensor", pairs)


def tensor_turn(value, tensor_count, step):
    width = tensor_count // Z_SIZE
    pairs = [
        (z * width + y, z * width + (y + step) % width)
        for z in range(Z_SIZE)
        for y in range(width)
    ]
    return lax.ppermute(value, "tensor", pairs)


def group_xor(value, group_count, bits):
    return lax.ppermute(value, "group", [(g, g ^ bits) for g in range(group_count)])


def own_quarter(block, prefix_owner, group_count):
    group = lax.axis_index("group")
    owner = prefix_owner[lax.axis_index("tensor")]
    rows = block.shape[0] // group_count
    quarter = block[:rows]
    for bits in range(1, group_count):
        came = group_xor(block[bits * rows : (bits + 1) * rows], group_count, bits)
        quarter = jnp.where(owner == (group ^ bits), came, quarter)
    return quarter


HBM = pl.BlockSpec(memory_space=pltpu.HBM)
ANYWHERE = pl.BlockSpec(memory_space=pl.ANY)


def whole(array):
    return pl.BlockSpec(array.shape, lambda *_: (0,) * len(array.shape))


def wholes(arrays):
    return [whole(array) for array in arrays]


def after(value, *earlier):
    return lax.optimization_barrier((value, *earlier))[0]


def swap_in_plane(value, x_core, group_count, tensor_count):
    pairs = []
    for group in range(group_count):
        for place in range(tensor_count):
            over_x = group % 2 == x_core
            target = (group ^ 2, place) if over_x else (group, place ^ 1)
            pairs.append((group * tensor_count + place, target[0] * tensor_count + target[1]))
    return lax.ppermute(value, ("group", "tensor"), pairs)


def plane_pair(value, group_count, tensor_count):
    if tensor_count != 2 * Z_SIZE:
        return [value, group_xor(value, group_count, 2)]
    return [value, swap_in_plane(value, 0, group_count, tensor_count)]


def plane_rest(pair, group_count, tensor_count):
    width = tensor_count // Z_SIZE
    if width != 2:
        return [tensor_turn(v, tensor_count, step) for step in range(1, width) for v in pair]
    return [swap_in_plane(v, 1, group_count, tensor_count) for v in pair]


def pack_kernel(side, w_in, w_down, inward, down, *halves):
    part = w_in.shape[2] // 2
    columns = pl.ds(pl.multiple_of(side[0] * part, part), part)
    for half in range(2):
        inward[:, half * part : (half + 1) * part] = w_in[half, :, columns]
    for block in range(down.shape[0] // part):
        down[block * part : (block + 1) * part, :] = w_down[
            columns, block * 2 * part : (block + 1) * 2 * part
        ]
    for step, out in enumerate(halves):

        @pl.when(pl.program_id(0) == step)
        def _():
            out[...] = inward[...]


def join_piece(gate, up, down):
    width = 2 * gate.shape[1]
    blocks = [down[:, at : at + width] for at in range(0, down.shape[1], width)]
    return jnp.concatenate([gate, up], axis=1), jnp.concatenate(blocks)


def split_piece(piece):
    inward, down = piece
    part = inward.shape[1] // 2
    blocks = [down[at : at + part] for at in range(0, down.shape[0], part)]
    return inward[:, :part], inward[:, part:], jnp.concatenate(blocks, axis=1)


def own_piece(w_in, w_down, side, halved):
    core = lax.axis_index("group") % 2
    depth, part = w_in.shape[1], w_in.shape[2] // 4
    if part % 128:
        start = (core * 2 + side) * part
        inward, down = join_piece(
            lax.dynamic_slice_in_dim(w_in[0], start, part, 1),
            lax.dynamic_slice_in_dim(w_in[1], start, part, 1),
            lax.dynamic_slice_in_dim(w_down, start, part, 0),
        )
        return [inward, down, inward[: depth // 2], inward[depth // 2 :]]
    shapes = [(depth, 2 * part), (depth // 2, 2 * part)]
    halves = [(depth // 2, 2 * part)] * (2 if halved else 0)
    return pl.pallas_call(
        pack_kernel,
        grid_spec=pltpu.PrefetchScalarGridSpec(
            num_scalar_prefetch=1,
            grid=(2,),
            in_specs=[
                pl.BlockSpec((2, depth // 2, 2 * part), lambda i, at: (0, i, at[1])),
                pl.BlockSpec((2 * part, depth // 2), lambda i, at: (at[1], i)),
            ],
            out_specs=[
                pl.BlockSpec((rows // 2, columns), lambda i, at: (i, 0)) for rows, columns in shapes
            ]
            + [pl.BlockSpec(shape, lambda i, at: (0, 0)) for shape in halves],
        ),
        out_shape=[jax.ShapeDtypeStruct(shape, w_in.dtype) for shape in shapes + halves],
        compiler_params=pltpu.CompilerParams(vmem_limit_bytes=60 << 20),
    )(jnp.stack([side, core]).astype(jnp.int32), w_in, w_down)


def merge_pieces(pieces):
    count = max(1, 128 // (pieces[0][0].shape[1] // 2))
    if count == 1:
        return pieces
    merged = []
    for at in range(0, len(pieces), count):
        joined = [(jnp.concatenate(p[:-1]), p[-1]) for p in pieces[at : at + count]]
        gates, ups, downs = zip(*[split_piece(p) for p in joined])
        merged.append(
            join_piece(
                jnp.concatenate(gates, axis=1),
                jnp.concatenate(ups, axis=1),
                jnp.concatenate(downs),
            )
        )
    return merged


def rms_norm(inputs, gain_row):
    floated = inputs.astype(jnp.float32)
    return (
        floated
        * lax.rsqrt(jnp.mean(floated * floated, axis=-1, keepdims=True) + EPSILON)
        * gain_row
    )


def positions(segment):
    row_number = segment.shape[0]
    row_index = jnp.arange(row_number, dtype=jnp.int32)
    same_request = segment[:, None] == segment[None, :]
    first_row = jnp.min(jnp.where(same_request, row_index[None, :], row_number), axis=1)
    return PREFIX_TOKENS + row_index - first_row


def rotary_tables(locate_position, width):
    half_dim = HEAD_DIMENSION // 2
    frequency = ROPE_BASE ** (-jnp.arange(half_dim, dtype=jnp.float32) / half_dim)
    angles = locate_position.astype(jnp.float32)[:, None] * frequency[None, :]
    cosine, sine = jnp.cos(angles), jnp.sin(angles)
    heads = width // HEAD_DIMENSION
    return jnp.tile(cosine, (1, 2 * heads)), jnp.tile(
        jnp.concatenate([-sine, sine], axis=1), (1, heads)
    )


def project_kernel(hidden, gain, weight, cosine, sine, *rest):
    out, normed = rest[-2:]
    step = pl.program_id(0)
    width = weight.shape[1]
    rotated_steps = (QUERY_HEADS + KEY_VALUE_HEADS) * HEAD_DIMENSION // width

    @pl.when(step == 0)
    def _():
        normed[...] = rms_norm(hidden[...], gain[...]).astype(jnp.bfloat16)

    projected = jnp.dot(normed[...], weight[...], preferred_element_type=jnp.float32)

    @pl.when(step < rotated_steps)
    def _():
        half_dim = HEAD_DIMENSION // 2
        lane = lax.broadcasted_iota(jnp.int32, projected.shape, 1)
        swapped = jnp.where(
            lane % HEAD_DIMENSION < half_dim,
            pltpu.roll(projected, width - half_dim, 1),
            pltpu.roll(projected, half_dim, 1),
        )
        heads = width // HEAD_DIMENSION
        cosines = jnp.concatenate([cosine[...]] * heads, axis=1)
        sines = jnp.concatenate([sine[...]] * heads, axis=1)
        out[...] = (projected * cosines + swapped * sines).astype(jnp.bfloat16)

    @pl.when(step >= rotated_steps)
    def _():
        out[...] = projected.astype(jnp.bfloat16)


def project(hidden_in, gain_row, weight, locate_position, earlier):
    rows, depth = hidden_in.shape
    columns = weight.shape[1]
    width = 8 * HEAD_DIMENSION
    cosine, sine = rotary_tables(locate_position, HEAD_DIMENSION)
    return pl.pallas_call(
        project_kernel,
        grid=(columns // width,),
        in_specs=[
            whole(hidden_in),
            whole(gain_row[None, :]),
            pl.BlockSpec((depth, width), lambda i: (0, i)),
            whole(cosine),
            whole(sine),
        ]
        + [pl.BlockSpec(memory_space=pl.ANY)] * len(earlier),
        out_specs=pl.BlockSpec((rows, width), lambda i: (0, i)),
        out_shape=jax.ShapeDtypeStruct((rows, columns), jnp.bfloat16),
        scratch_shapes=[pltpu.VMEM((rows, depth), jnp.bfloat16)],
        compiler_params=pltpu.CompilerParams(vmem_limit_bytes=60 << 20),
        cost_estimate=pl.CostEstimate(
            flops=2 * rows * depth * columns,
            bytes_accessed=2 * depth * columns,
            transcendentals=0,
        ),
    )(hidden_in, gain_row[None, :], weight, cosine, sine, *earlier)


def head_columns(index):
    return slice(index * HEAD_DIMENSION, (index + 1) * HEAD_DIMENSION)


def attention_kernel(piece_count, heads, row_ids, column_ids, projected, *rest):
    pieces, out, joined, semaphores = rest[:piece_count], *rest[-3:]
    rows = projected.shape[0]
    repeats = QUERY_HEADS // KEY_VALUE_HEADS
    first, count = heads
    width = count * HEAD_DIMENSION
    key_value_width = KEY_VALUE_HEADS * HEAD_DIMENSION
    copies, at = [], 0
    for index, piece in enumerate(pieces):
        for side in range(2):
            start = side * key_value_width + first * HEAD_DIMENSION
            source = piece.at[:, pl.ds(start, width)]
            target = joined.at[pl.ds(at, piece.shape[0]), pl.ds(side * width, width)]
            copies.append(pltpu.make_async_copy(source, target, semaphores.at[2 * index + side]))
        at += piece.shape[0]
    for copy in copies:
        copy.start()
    for side in range(2):
        start = (QUERY_HEADS + side * KEY_VALUE_HEADS + first) * HEAD_DIMENSION
        joined[at : at + rows, side * width : (side + 1) * width] = projected[
            :, start : start + width
        ]
    row_index = lax.broadcasted_iota(jnp.int32, (rows, rows), 0)
    column_index = lax.broadcasted_iota(jnp.int32, (rows, rows), 1)
    allowed = (row_ids[...] == column_ids[...]) & (column_index <= row_index)
    allowed = jnp.concatenate([allowed] * repeats, axis=0)
    scale = HEAD_DIMENSION ** (-0.5) * LOG2_E
    for copy in copies:
        copy.wait()
    for head in range(count):
        queries = jnp.concatenate(
            [projected[:, head_columns((first + head) * repeats + g)] for g in range(repeats)],
            axis=0,
        )
        scores = lax.dot_general(
            queries,
            joined[:, head_columns(head)],
            (((1,), (1,)), ((), ())),
            preferred_element_type=jnp.float32,
        )
        scores = jnp.concatenate(
            [scores[:, :at], jnp.where(allowed, scores[:, at:], NEGATIVE_FILLER)], axis=1
        )
        top = jnp.max(scores, axis=1, keepdims=True)
        weights = jnp.exp2((scores - top) * scale)
        total = jnp.sum(weights, axis=1, keepdims=True)
        summed = jnp.dot(
            weights.astype(jnp.bfloat16),
            joined[:, head_columns(count + head)],
            preferred_element_type=jnp.float32,
        )
        attended = (summed / total).astype(jnp.bfloat16)
        for g in range(repeats):
            out[:, head_columns(head * repeats + g)] = attended[g * rows : (g + 1) * rows]


def last_attention_kernel(
    piece_count, heads, row_ids, column_ids, projected, hidden, gain, *rest
):
    pieces, w_out = rest[:piece_count], rest[piece_count]
    middle, second, joined, semaphores, out, weight, semaphore = rest[-7:]
    fetch = pltpu.make_async_copy(w_out, weight, semaphore)
    fetch.start()
    attention_kernel(
        piece_count, heads, row_ids, column_ids, projected, *pieces, out, joined, semaphores
    )
    fetch.wait()
    added = jnp.dot(out[...], weight[...], preferred_element_type=jnp.float32)
    middle[...] = (hidden[...].astype(jnp.float32) + added).astype(jnp.bfloat16)
    second[...] = rms_norm(middle[...], gain[...]).astype(jnp.bfloat16)


def attend(segment, projected, pieces, heads, rest=None):
    rows = projected.shape[0]
    key_count = rows + sum(piece.shape[0] for piece in pieces)
    width = heads[1] * HEAD_DIMENSION
    columns = width * QUERY_HEADS // KEY_VALUE_HEADS
    resident = [segment[:, None], segment[None, :], projected]
    remote = list(pieces)
    kernel = attention_kernel
    out = [jax.ShapeDtypeStruct((rows, columns), jnp.bfloat16)]
    scratch = [
        pltpu.VMEM((key_count, 2 * width), jnp.bfloat16),
        pltpu.SemaphoreType.DMA((2 * len(pieces),)),
    ]
    if rest is not None:
        hidden_in, gain_row, w_out = rest
        resident += [hidden_in, gain_row[None, :]]
        remote.append(w_out)
        kernel = last_attention_kernel
        out = [jax.ShapeDtypeStruct(hidden_in.shape, jnp.bfloat16)] * 2
        scratch += [
            pltpu.VMEM((rows, columns), jnp.bfloat16),
            pltpu.VMEM(w_out.shape, jnp.bfloat16),
            pltpu.SemaphoreType.DMA,
        ]
    return pl.pallas_call(
        functools.partial(kernel, len(pieces), heads),
        grid=(1,),
        in_specs=wholes(resident) + [HBM] * len(remote),
        out_specs=wholes(out),
        out_shape=out,
        scratch_shapes=scratch,
        compiler_params=pltpu.CompilerParams(vmem_limit_bytes=60 << 20),
    )(*resident, *remote)


def feed_forward_kernel(chunks, piece_count, carry_count, left, right, *rest):
    weights = rest[: chunks * piece_count]
    carries = rest[chunks * piece_count : chunks * piece_count + carry_count]
    left_out, right_out, tokens, acts = rest[-4:]
    rows, depth = left.shape
    part = weights[0].shape[1] // 2
    tokens[:rows, :] = left[...]
    tokens[rows:, :] = right[...]
    for index in range(piece_count):
        both, at = 0.0, 0
        for weight in weights[chunks * index : chunks * (index + 1) - 1]:
            columns = slice(at, at + weight.shape[0])
            both += jnp.dot(
                tokens[:, columns], weight[...], preferred_element_type=jnp.float32
            )
            at += weight.shape[0]
        gate, up = both[:, :part], both[:, part:]
        acts[:, index * part : (index + 1) * part] = (gate / (1.0 + jnp.exp(-gate)) * up).astype(
            jnp.bfloat16
        )
    for block in range(depth // (2 * part)):
        columns = slice(block * 2 * part, (block + 1) * 2 * part)
        weight = jnp.concatenate(
            [v[block * part : (block + 1) * part, :] for v in weights[chunks - 1 :: chunks]]
        )
        sums = jnp.dot(acts[...], weight, preferred_element_type=jnp.float32)
        for side, out in enumerate((left_out, right_out)):
            found = sums[side * rows : (side + 1) * rows]
            for carry in carries[side::2]:
                found += carry[:, columns].astype(jnp.float32)
            out[:, columns] = found.astype(out.dtype)


def feed_forward(left, right, pieces, carries, right_dtype, earlier=()):
    rows, depth = left.shape
    part = pieces[0][0].shape[1] // 2
    chunks = [chunk for piece in pieces for chunk in piece]
    out = [jax.ShapeDtypeStruct((rows, depth), dtype) for dtype in (jnp.float32, right_dtype)]
    return pl.pallas_call(
        functools.partial(feed_forward_kernel, len(pieces[0]), len(pieces), len(carries)),
        grid=(1,),
        in_specs=wholes([left, right, *chunks, *carries]) + [ANYWHERE] * len(earlier),
        out_specs=wholes(out),
        out_shape=out,
        scratch_shapes=[
            pltpu.VMEM((2 * rows, depth), jnp.bfloat16),
            pltpu.VMEM((2 * rows, part * len(pieces)), jnp.bfloat16),
        ],
        compiler_params=pltpu.CompilerParams(vmem_limit_bytes=32 << 20),
    )(left, right, *chunks, *carries, *earlier)


def add_rows(first, *others):
    arrays = [first, *others]
    rows, columns = first.shape
    block = pl.BlockSpec((rows // 4, columns), lambda i: (i, 0))

    def kernel(*refs):
        refs[-1][...] = sum(ref[...].astype(jnp.float32) for ref in refs[:-1]).astype(jnp.bfloat16)

    return pl.pallas_call(
        kernel,
        grid=(4,),
        in_specs=[block] * len(arrays),
        out_specs=block,
        out_shape=jax.ShapeDtypeStruct(first.shape, jnp.bfloat16),
    )(*arrays)


def select_kernel(group_count, table, projected, *rest):
    outs = rest[-group_count:]
    page_rows = outs[0].shape[0] // CAP
    columns = outs[0].shape[1]
    for index in range(group_count * CAP):
        page = table[index]
        start = pl.multiple_of(jnp.maximum(page, 0) * page_rows, page_rows)
        rows = projected[pl.ds(start, page_rows), columns:]
        slot = index % CAP
        outs[index // CAP][slot * page_rows : (slot + 1) * page_rows, :] = jnp.where(
            page >= 0, rows, jnp.zeros_like(rows)
        )


def select_pages(projected, destination, group_count, earlier):
    page_count = destination.shape[0]
    page_rows = projected.shape[0] // page_count
    group = lax.axis_index("group")
    same = destination[:, None] == destination[None, :]
    page = jnp.arange(page_count, dtype=jnp.int32)
    rank = jnp.sum(same & (page[None, :] < page[:, None]), axis=1, dtype=jnp.int32)
    slot = (destination ^ group) * CAP + rank
    chosen = slot[None, :] == jnp.arange(group_count * CAP, dtype=jnp.int32)[:, None]
    table = jnp.max(jnp.where(chosen, page[None, :], -1), axis=1)
    columns = projected.shape[1] // 2
    out = [jax.ShapeDtypeStruct((CAP * page_rows, columns), projected.dtype)] * group_count
    return pl.pallas_call(
        functools.partial(select_kernel, group_count),
        grid_spec=pltpu.PrefetchScalarGridSpec(
            num_scalar_prefetch=1,
            grid=(1,),
            in_specs=[whole(projected)] + [ANYWHERE] * len(earlier),
            out_specs=wholes(out),
        ),
        out_shape=out,
        compiler_params=pltpu.CompilerParams(vmem_limit_bytes=16 << 20),
    )(table, projected, *earlier)


def place_kernel(group, *rest):
    *received, out = rest
    for bits, block in enumerate(received):
        out[group[0] ^ bits] = block[...]


def place_pages(received):
    out = jax.ShapeDtypeStruct((len(received), *received[0].shape), received[0].dtype)
    return pl.pallas_call(
        place_kernel,
        grid_spec=pltpu.PrefetchScalarGridSpec(
            num_scalar_prefetch=1,
            grid=(1,),
            in_specs=wholes(received),
            out_specs=whole(out),
        ),
        out_shape=out,
    )(lax.axis_index("group")[None].astype(jnp.int32), *received)


def on_device(
    hidden_in,
    request_ids,
    norm_gains,
    query_key_value_weight,
    w_out,
    w_in,
    w_down,
    prefix_cache,
    prefix_owner,
    page_dest,
):
    group_count, tensor_count = lax.axis_size("group"), lax.axis_size("tensor")
    sizes = (group_count, tensor_count)
    turns = range(1, tensor_count // Z_SIZE)
    segment = request_ids[0]
    quarter = own_quarter(prefix_cache[0], prefix_owner, group_count)
    across = lax.axis_index("group") // 2
    *mine, upper, lower = own_piece(w_in, w_down, across, True)
    far_down = tensor_xor(mine[1], tensor_count, 2)
    beside = [[tensor_turn(v, tensor_count, step) for v in mine] for step in turns]
    along_z = [tensor_xor(quarter, tensor_count, bits) for bits in range(1, Z_SIZE)]
    projected = project(
        after(hidden_in, mine[0], quarter),
        norm_gains[0],
        query_key_value_weight,
        positions(after(segment, quarter)),
        [],
    )
    line = after(jnp.concatenate([quarter] + along_z), projected, far_down)
    other = own_piece(w_in, w_down, after(1 - across, projected), False)[:2]
    far_upper = tensor_xor(after(upper, line), tensor_count, 2)
    lines = plane_pair(line, *sizes)
    across = [[group_xor(v, group_count, 2) for v in pair] for pair in beside]
    lines = after(jnp.concatenate(lines), beside[0][1], across[0][0], other[1], far_upper)
    lines = [lines] + plane_rest([lines], *sizes)
    down_pair = plane_pair(far_down, *sizes)
    near = [pair for pairs in zip(beside, across) for pair in pairs]
    lines += [
        group_xor(lines[0], group_count, 1),
        *[group_xor(v, group_count, 1) for v in lines[1:]],
    ]
    far_lower = tensor_xor(after(lower, far_upper), tensor_count, 2)
    upper_pair = plane_pair(far_upper, *sizes)
    middle, second = attend(
        segment,
        projected,
        lines,
        (0, KEY_VALUE_HEADS),
        (hidden_in, norm_gains[1], w_out),
    )
    far = after(second, far_lower, upper_pair[1], down_pair[1], across[0][1])
    far = tensor_xor(far, tensor_count, 1)
    late_down = down_pair + plane_rest(down_pair, *sizes)
    late_upper = upper_pair + plane_rest(upper_pair, *sizes)
    lower_pair = plane_pair(far_lower, *sizes)
    late_lower = lower_pair + plane_rest(lower_pair, *sizes)
    late = list(zip(late_upper, late_lower, late_down))
    beside = group_xor(second, group_count, 1)
    near = merge_pieces([mine, other] + near)
    late = merge_pieces(late)
    own_early = feed_forward(second, beside, near, [], jnp.float32)
    far_beside = group_xor(
        after(far, own_early[0], lower_pair[1], *late_down[2:], *late_upper[2:]), group_count, 1
    )
    far_early = feed_forward(far, far_beside, near, [], jnp.float32, own_early)
    outgoing = select_pages(projected, page_dest[:, 0], group_count, [far])
    far_sum, far_beside_sum = feed_forward(
        far, far_beside, late, far_early, jnp.bfloat16, [outgoing[0]]
    )
    far_sum = far_sum + group_xor(far_beside_sum, group_count, 1).astype(jnp.float32)
    far_sum = far_sum.astype(jnp.bfloat16)
    returned = tensor_xor(far_sum, tensor_count, 1)
    received = [outgoing[0], group_xor(after(outgoing[1], far_sum), group_count, 1)]
    received += [
        group_xor(outgoing[bits], group_count, bits) for bits in range(2, group_count)
    ]
    own_sum, beside_sum = feed_forward(
        after(second, far_sum, received[1]), beside, late, [*own_early, middle], jnp.bfloat16
    )
    received = place_pages(received)
    own_beside = group_xor(after(beside_sum, received), group_count, 1)
    hidden_out = add_rows(own_sum, own_beside, after(returned, received))
    pages = received.reshape(group_count, CAP, -1, received.shape[2])
    return (hidden_out, pages[None, None])


def solution(mesh):
    return jax.shard_map(
        on_device,
        mesh=mesh,
        in_specs=(
            P(("group", "tensor"), None),
            P(("group", "tensor"), None),
            P(),
            P(),
            P(),
            P(None, None, "tensor"),
            P("tensor", None),
            P("group", "tensor", None),
            P(),
            P(("group", "tensor"), None),
        ),
        out_specs=(P(("group", "tensor"), None), P("group", "tensor", None, None, None, None)),
        check_vma=False,
    )
```

```python
import functools

import jax
import jax.numpy as jnp
from jax import lax
from jax.experimental import pallas as pl
from jax.experimental.pallas import tpu as pltpu
from jax.sharding import PartitionSpec as P

QUERY_HEADS = 16
KEY_VALUE_HEADS = 8
HEAD_DIMENSION = 96
PREFIX_TOKENS = 1024
CAP = 8


ROPE_BASE = 100000.0
EPSILON = 1e-05
NEGATIVE_FILLER = -1e30
LOG2_E = 1.4426950408889634


Z_SIZE = 4


def tensor_xor(value, tensor_count, z_bits):
    width = tensor_count // Z_SIZE
    pairs = [
        (z * width + y, (z ^ z_bits) * width + y) for z in range(Z_SIZE) for y in range(width)
    ]
    return lax.ppermute(value, "tensor", pairs)


def tensor_turn(value, tensor_count, step):
    width = tensor_count // Z_SIZE
    pairs = [
        (z * width + y, z * width + (y + step) % width)
        for z in range(Z_SIZE)
        for y in range(width)
    ]
    return lax.ppermute(value, "tensor", pairs)


def group_xor(value, group_count, bits):
    return lax.ppermute(value, "group", [(g, g ^ bits) for g in range(group_count)])


def own_quarter(block, prefix_owner, group_count):
    group = lax.axis_index("group")
    owner = prefix_owner[lax.axis_index("tensor")]
    rows = block.shape[0] // group_count
    quarter = block[:rows]
    for bits in range(1, group_count):
        came = group_xor(block[bits * rows : (bits + 1) * rows], group_count, bits)
        quarter = jnp.where(owner == (group ^ bits), came, quarter)
    return quarter


HBM = pl.BlockSpec(memory_space=pltpu.HBM)
ANYWHERE = pl.BlockSpec(memory_space=pl.ANY)


def whole(array):
    return pl.BlockSpec(array.shape, lambda *_: (0,) * len(array.shape))


def wholes(arrays):
    return [whole(array) for array in arrays]


def after(value, *earlier):
    return lax.optimization_barrier((value, *earlier))[0]


def swap_in_plane(value, x_core, group_count, tensor_count):
    pairs = []
    for group in range(group_count):
        for place in range(tensor_count):
            over_x = group % 2 == x_core
            target = (group ^ 2, place) if over_x else (group, place ^ 1)
            pairs.append((group * tensor_count + place, target[0] * tensor_count + target[1]))
    return lax.ppermute(value, ("group", "tensor"), pairs)


def plane_pair(value, group_count, tensor_count):
    if tensor_count != 2 * Z_SIZE:
        return [value, group_xor(value, group_count, 2)]
    return [value, swap_in_plane(value, 0, group_count, tensor_count)]


def plane_rest(pair, group_count, tensor_count):
    width = tensor_count // Z_SIZE
    if width != 2:
        return [tensor_turn(v, tensor_count, step) for step in range(1, width) for v in pair]
    return [swap_in_plane(v, 1, group_count, tensor_count) for v in pair]


def pack_kernel(side, w_in, w_down, inward, down, *halves):
    part = w_in.shape[2] // 2
    columns = pl.ds(pl.multiple_of(side[0] * part, part), part)
    for half in range(2):
        inward[:, half * part : (half + 1) * part] = w_in[half, :, columns]
    for block in range(down.shape[0] // part):
        down[block * part : (block + 1) * part, :] = w_down[
            columns, block * 2 * part : (block + 1) * 2 * part
        ]
    for step, out in enumerate(halves):

        @pl.when(pl.program_id(0) == step)
        def _():
            out[...] = inward[...]


def join_piece(gate, up, down):
    width = 2 * gate.shape[1]
    blocks = [down[:, at : at + width] for at in range(0, down.shape[1], width)]
    return jnp.concatenate([gate, up], axis=1), jnp.concatenate(blocks)


def split_piece(piece):
    inward, down = piece
    part = inward.shape[1] // 2
    blocks = [down[at : at + part] for at in range(0, down.shape[0], part)]
    return inward[:, :part], inward[:, part:], jnp.concatenate(blocks, axis=1)


def own_piece(w_in, w_down, side, halved):
    core = lax.axis_index("group") % 2
    depth, part = w_in.shape[1], w_in.shape[2] // 4
    if part % 128:
        start = (core * 2 + side) * part
        inward, down = join_piece(
            lax.dynamic_slice_in_dim(w_in[0], start, part, 1),
            lax.dynamic_slice_in_dim(w_in[1], start, part, 1),
            lax.dynamic_slice_in_dim(w_down, start, part, 0),
        )
        return [inward, down, inward[: depth // 2], inward[depth // 2 :]]
    shapes = [(depth, 2 * part), (depth // 2, 2 * part)]
    halves = [(depth // 2, 2 * part)] * (2 if halved else 0)
    return pl.pallas_call(
        pack_kernel,
        grid_spec=pltpu.PrefetchScalarGridSpec(
            num_scalar_prefetch=1,
            grid=(2,),
            in_specs=[
                pl.BlockSpec((2, depth // 2, 2 * part), lambda i, at: (0, i, at[1])),
                pl.BlockSpec((2 * part, depth // 2), lambda i, at: (at[1], i)),
            ],
            out_specs=[
                pl.BlockSpec((rows // 2, columns), lambda i, at: (i, 0)) for rows, columns in shapes
            ]
            + [pl.BlockSpec(shape, lambda i, at: (0, 0)) for shape in halves],
        ),
        out_shape=[jax.ShapeDtypeStruct(shape, w_in.dtype) for shape in shapes + halves],
        compiler_params=pltpu.CompilerParams(vmem_limit_bytes=60 << 20),
    )(jnp.stack([side, core]).astype(jnp.int32), w_in, w_down)


def halves_of(arrays):
    return [(array, half) for array in arrays for half in range(2)]


def block_of(chunk):
    if not isinstance(chunk, tuple):
        return whole(chunk)
    array, half = chunk
    return pl.BlockSpec((array.shape[0] // 2, array.shape[1]), lambda *_: (half, 0))


def rows_of(chunk):
    if not isinstance(chunk, tuple):
        return chunk
    array, half = chunk
    return jnp.split(array, 2)[half]


def merge_pieces(pieces):
    count = max(1, 128 // (pieces[0][0].shape[1] // 2))
    if count == 1:
        return pieces
    merged = []
    for at in range(0, len(pieces), count):
        taken = [[rows_of(chunk) for chunk in p] for p in pieces[at : at + count]]
        joined = [(jnp.concatenate(p[:-1]), p[-1]) for p in taken]
        gates, ups, downs = zip(*[split_piece(p) for p in joined])
        merged.append(
            join_piece(
                jnp.concatenate(gates, axis=1),
                jnp.concatenate(ups, axis=1),
                jnp.concatenate(downs),
            )
        )
    return merged


def rms_norm(inputs, gain_row):
    floated = inputs.astype(jnp.float32)
    return (
        floated
        * lax.rsqrt(jnp.mean(floated * floated, axis=-1, keepdims=True) + EPSILON)
        * gain_row
    )


def positions(segment):
    row_number = segment.shape[0]
    row_index = jnp.arange(row_number, dtype=jnp.int32)
    same_request = segment[:, None] == segment[None, :]
    first_row = jnp.min(jnp.where(same_request, row_index[None, :], row_number), axis=1)
    return PREFIX_TOKENS + row_index - first_row


def rotary_tables(locate_position, width):
    half_dim = HEAD_DIMENSION // 2
    frequency = ROPE_BASE ** (-jnp.arange(half_dim, dtype=jnp.float32) / half_dim)
    angles = locate_position.astype(jnp.float32)[:, None] * frequency[None, :]
    cosine, sine = jnp.cos(angles), jnp.sin(angles)
    heads = width // HEAD_DIMENSION
    return jnp.tile(cosine, (1, 2 * heads)), jnp.tile(
        jnp.concatenate([-sine, sine], axis=1), (1, heads)
    )


def project_kernel(hidden, gain, weight, cosine, sine, *rest):
    out, normed = rest[-2:]
    step = pl.program_id(0)
    width = weight.shape[1]
    rotated_steps = (QUERY_HEADS + KEY_VALUE_HEADS) * HEAD_DIMENSION // width

    @pl.when(step == 0)
    def _():
        normed[...] = rms_norm(hidden[...], gain[...]).astype(jnp.bfloat16)

    projected = jnp.dot(normed[...], weight[...], preferred_element_type=jnp.float32)

    @pl.when(step < rotated_steps)
    def _():
        half_dim = HEAD_DIMENSION // 2
        lane = lax.broadcasted_iota(jnp.int32, projected.shape, 1)
        swapped = jnp.where(
            lane % HEAD_DIMENSION < half_dim,
            pltpu.roll(projected, width - half_dim, 1),
            pltpu.roll(projected, half_dim, 1),
        )
        heads = width // HEAD_DIMENSION
        cosines = jnp.concatenate([cosine[...]] * heads, axis=1)
        sines = jnp.concatenate([sine[...]] * heads, axis=1)
        out[...] = (projected * cosines + swapped * sines).astype(jnp.bfloat16)

    @pl.when(step >= rotated_steps)
    def _():
        out[...] = projected.astype(jnp.bfloat16)


def project(hidden_in, gain_row, weight, locate_position, earlier):
    rows, depth = hidden_in.shape
    columns = weight.shape[1]
    width = 8 * HEAD_DIMENSION
    cosine, sine = rotary_tables(locate_position, HEAD_DIMENSION)
    return pl.pallas_call(
        project_kernel,
        grid=(columns // width,),
        in_specs=[
            whole(hidden_in),
            whole(gain_row[None, :]),
            pl.BlockSpec((depth, width), lambda i: (0, i)),
            whole(cosine),
            whole(sine),
        ]
        + [pl.BlockSpec(memory_space=pl.ANY)] * len(earlier),
        out_specs=pl.BlockSpec((rows, width), lambda i: (0, i)),
        out_shape=jax.ShapeDtypeStruct((rows, columns), jnp.bfloat16),
        scratch_shapes=[pltpu.VMEM((rows, depth), jnp.bfloat16)],
        compiler_params=pltpu.CompilerParams(vmem_limit_bytes=60 << 20),
        cost_estimate=pl.CostEstimate(
            flops=2 * rows * depth * columns,
            bytes_accessed=2 * depth * columns,
            transcendentals=0,
        ),
    )(hidden_in, gain_row[None, :], weight, cosine, sine, *earlier)


def head_columns(index):
    return slice(index * HEAD_DIMENSION, (index + 1) * HEAD_DIMENSION)


def attention_kernel(piece_count, heads, row_ids, column_ids, projected, *rest):
    pieces, out, joined, semaphores = rest[:piece_count], *rest[-3:]
    rows = projected.shape[0]
    repeats = QUERY_HEADS // KEY_VALUE_HEADS
    first, count = heads
    width = count * HEAD_DIMENSION
    key_value_width = KEY_VALUE_HEADS * HEAD_DIMENSION
    copies, at = [], 0
    for index, piece in enumerate(pieces):
        for side in range(2):
            start = side * key_value_width + first * HEAD_DIMENSION
            source = piece.at[:, pl.ds(start, width)]
            target = joined.at[pl.ds(at, piece.shape[0]), pl.ds(side * width, width)]
            copies.append(pltpu.make_async_copy(source, target, semaphores.at[2 * index + side]))
        at += piece.shape[0]
    for copy in copies:
        copy.start()
    for side in range(2):
        start = (QUERY_HEADS + side * KEY_VALUE_HEADS + first) * HEAD_DIMENSION
        joined[at : at + rows, side * width : (side + 1) * width] = projected[
            :, start : start + width
        ]
    row_index = lax.broadcasted_iota(jnp.int32, (rows, rows), 0)
    column_index = lax.broadcasted_iota(jnp.int32, (rows, rows), 1)
    allowed = (row_ids[...] == column_ids[...]) & (column_index <= row_index)
    allowed = jnp.concatenate([allowed] * repeats, axis=0)
    scale = HEAD_DIMENSION ** (-0.5) * LOG2_E
    for copy in copies:
        copy.wait()
    for head in range(count):
        queries = jnp.concatenate(
            [projected[:, head_columns((first + head) * repeats + g)] for g in range(repeats)],
            axis=0,
        )
        scores = lax.dot_general(
            queries,
            joined[:, head_columns(head)],
            (((1,), (1,)), ((), ())),
            preferred_element_type=jnp.float32,
        )
        scores = jnp.concatenate(
            [scores[:, :at], jnp.where(allowed, scores[:, at:], NEGATIVE_FILLER)], axis=1
        )
        top = jnp.max(scores, axis=1, keepdims=True)
        weights = jnp.exp2((scores - top) * scale)
        total = jnp.sum(weights, axis=1, keepdims=True)
        summed = jnp.dot(
            weights.astype(jnp.bfloat16),
            joined[:, head_columns(count + head)],
            preferred_element_type=jnp.float32,
        )
        attended = (summed / total).astype(jnp.bfloat16)
        for g in range(repeats):
            out[:, head_columns(head * repeats + g)] = attended[g * rows : (g + 1) * rows]


def last_attention_kernel(
    piece_count, heads, row_ids, column_ids, projected, hidden, gain, *rest
):
    pieces, w_out = rest[:piece_count], rest[piece_count]
    middle, second, joined, semaphores, out, weight, semaphore = rest[-7:]
    fetch = pltpu.make_async_copy(w_out, weight, semaphore)
    fetch.start()
    attention_kernel(
        piece_count, heads, row_ids, column_ids, projected, *pieces, out, joined, semaphores
    )
    fetch.wait()
    added = jnp.dot(out[...], weight[...], preferred_element_type=jnp.float32)
    middle[...] = (hidden[...].astype(jnp.float32) + added).astype(jnp.bfloat16)
    second[...] = rms_norm(middle[...], gain[...]).astype(jnp.bfloat16)


def attend(segment, projected, pieces, heads, rest=None):
    rows = projected.shape[0]
    key_count = rows + sum(piece.shape[0] for piece in pieces)
    width = heads[1] * HEAD_DIMENSION
    columns = width * QUERY_HEADS // KEY_VALUE_HEADS
    resident = [segment[:, None], segment[None, :], projected]
    remote = list(pieces)
    kernel = attention_kernel
    out = [jax.ShapeDtypeStruct((rows, columns), jnp.bfloat16)]
    scratch = [
        pltpu.VMEM((key_count, 2 * width), jnp.bfloat16),
        pltpu.SemaphoreType.DMA((2 * len(pieces),)),
    ]
    if rest is not None:
        hidden_in, gain_row, w_out = rest
        resident += [hidden_in, gain_row[None, :]]
        remote.append(w_out)
        kernel = last_attention_kernel
        out = [jax.ShapeDtypeStruct(hidden_in.shape, jnp.bfloat16)] * 2
        scratch += [
            pltpu.VMEM((rows, columns), jnp.bfloat16),
            pltpu.VMEM(w_out.shape, jnp.bfloat16),
            pltpu.SemaphoreType.DMA,
        ]
    return pl.pallas_call(
        functools.partial(kernel, len(pieces), heads),
        grid=(1,),
        in_specs=wholes(resident) + [HBM] * len(remote),
        out_specs=wholes(out),
        out_shape=out,
        scratch_shapes=scratch,
        compiler_params=pltpu.CompilerParams(vmem_limit_bytes=60 << 20),
    )(*resident, *remote)


def feed_forward_kernel(chunks, piece_count, carry_count, left, right, *rest):
    weights = rest[: chunks * piece_count]
    carries = rest[chunks * piece_count : chunks * piece_count + carry_count]
    left_out, right_out, tokens, acts = rest[-4:]
    rows, depth = left.shape
    part = weights[0].shape[1] // 2
    tokens[:rows, :] = left[...]
    tokens[rows:, :] = right[...]
    for index in range(piece_count):
        both, at = 0.0, 0
        for weight in weights[chunks * index : chunks * (index + 1) - 1]:
            columns = slice(at, at + weight.shape[0])
            both += jnp.dot(
                tokens[:, columns], weight[...], preferred_element_type=jnp.float32
            )
            at += weight.shape[0]
        gate, up = both[:, :part], both[:, part:]
        acts[:, index * part : (index + 1) * part] = (gate / (1.0 + jnp.exp(-gate)) * up).astype(
            jnp.bfloat16
        )
    for block in range(depth // (2 * part)):
        columns = slice(block * 2 * part, (block + 1) * 2 * part)
        weight = jnp.concatenate(
            [v[block * part : (block + 1) * part, :] for v in weights[chunks - 1 :: chunks]]
        )
        sums = jnp.dot(acts[...], weight, preferred_element_type=jnp.float32)
        for side, out in enumerate((left_out, right_out)):
            found = sums[side * rows : (side + 1) * rows]
            for carry in carries[side::2]:
                found += carry[:, columns].astype(jnp.float32)
            out[:, columns] = found.astype(out.dtype)


def feed_forward(left, right, pieces, carries, right_dtype, earlier=()):
    rows, depth = left.shape
    part = pieces[0][0].shape[1] // 2
    chunks = [chunk for piece in pieces for chunk in piece]
    blocks = [block_of(chunk) for chunk in chunks]
    chunks = [chunk[0] if isinstance(chunk, tuple) else chunk for chunk in chunks]
    out = [jax.ShapeDtypeStruct((rows, depth), dtype) for dtype in (jnp.float32, right_dtype)]
    return pl.pallas_call(
        functools.partial(feed_forward_kernel, len(pieces[0]), len(pieces), len(carries)),
        grid=(1,),
        in_specs=[
            *wholes([left, right]),
            *blocks,
            *wholes(carries),
            *[ANYWHERE] * len(earlier),
        ],
        out_specs=wholes(out),
        out_shape=out,
        scratch_shapes=[
            pltpu.VMEM((2 * rows, depth), jnp.bfloat16),
            pltpu.VMEM((2 * rows, part * len(pieces)), jnp.bfloat16),
        ],
        compiler_params=pltpu.CompilerParams(vmem_limit_bytes=32 << 20),
    )(left, right, *chunks, *carries, *earlier)


def add_rows(first, *others):
    arrays = [first, *others]
    def kernel(*refs):
        refs[-1][...] = sum(ref[...].astype(jnp.float32) for ref in refs[:-1]).astype(jnp.bfloat16)

    return pl.pallas_call(
        kernel,
        grid=(1,),
        in_specs=wholes(arrays),
        out_specs=whole(first),
        out_shape=jax.ShapeDtypeStruct(first.shape, jnp.bfloat16),
    )(*arrays)


def select_kernel(group_count, table, projected, *rest):
    outs = rest[-group_count:]
    page_rows = outs[0].shape[0] // CAP
    columns = outs[0].shape[1]
    for index in range(group_count * CAP):
        page = table[index]
        start = pl.multiple_of(jnp.maximum(page, 0) * page_rows, page_rows)
        rows = projected[pl.ds(start, page_rows), columns:]
        slot = index % CAP
        outs[index // CAP][slot * page_rows : (slot + 1) * page_rows, :] = jnp.where(
            page >= 0, rows, jnp.zeros_like(rows)
        )


def select_pages(projected, destination, group_count, earlier):
    page_count = destination.shape[0]
    page_rows = projected.shape[0] // page_count
    group = lax.axis_index("group")
    same = destination[:, None] == destination[None, :]
    page = jnp.arange(page_count, dtype=jnp.int32)
    rank = jnp.sum(same & (page[None, :] < page[:, None]), axis=1, dtype=jnp.int32)
    slot = (destination ^ group) * CAP + rank
    chosen = slot[None, :] == jnp.arange(group_count * CAP, dtype=jnp.int32)[:, None]
    table = jnp.max(jnp.where(chosen, page[None, :], -1), axis=1)
    columns = projected.shape[1] // 2
    out = [jax.ShapeDtypeStruct((CAP * page_rows, columns), projected.dtype)] * group_count
    return pl.pallas_call(
        functools.partial(select_kernel, group_count),
        grid_spec=pltpu.PrefetchScalarGridSpec(
            num_scalar_prefetch=1,
            grid=(1,),
            in_specs=[whole(projected)] + [ANYWHERE] * len(earlier),
            out_specs=wholes(out),
        ),
        out_shape=out,
        compiler_params=pltpu.CompilerParams(vmem_limit_bytes=16 << 20),
    )(table, projected, *earlier)


def place_kernel(group, *rest):
    *received, out = rest
    for bits, block in enumerate(received):
        out[group[0] ^ bits] = block[...]


def place_pages(received):
    out = jax.ShapeDtypeStruct((len(received), *received[0].shape), received[0].dtype)
    return pl.pallas_call(
        place_kernel,
        grid_spec=pltpu.PrefetchScalarGridSpec(
            num_scalar_prefetch=1,
            grid=(1,),
            in_specs=wholes(received),
            out_specs=whole(out),
        ),
        out_shape=out,
    )(lax.axis_index("group")[None].astype(jnp.int32), *received)


def on_device(
    hidden_in,
    request_ids,
    norm_gains,
    query_key_value_weight,
    w_out,
    w_in,
    w_down,
    prefix_cache,
    prefix_owner,
    page_dest,
):
    group_count, tensor_count = lax.axis_size("group"), lax.axis_size("tensor")
    sizes = (group_count, tensor_count)
    turns = range(1, tensor_count // Z_SIZE)
    segment = request_ids[0]
    quarter = own_quarter(prefix_cache[0], prefix_owner, group_count)
    across = lax.axis_index("group") // 2
    *mine, upper, lower = own_piece(w_in, w_down, across, True)
    far_down = tensor_xor(mine[1], tensor_count, 2)
    beside = [[tensor_turn(v, tensor_count, step) for v in mine] for step in turns]
    along_z = [tensor_xor(quarter, tensor_count, bits) for bits in range(1, Z_SIZE)]
    projected = project(
        after(hidden_in, mine[0], quarter),
        norm_gains[0],
        query_key_value_weight,
        positions(after(segment, quarter)),
        [],
    )
    line = after(jnp.concatenate([quarter] + along_z), projected, far_down)
    other = own_piece(w_in, w_down, after(1 - across, projected), False)[:2]
    far_upper = tensor_xor(after(upper, line), tensor_count, 2)
    lines = plane_pair(line, *sizes)
    across = [[group_xor(v, group_count, 2) for v in pair] for pair in beside]
    down_pair = plane_pair(far_down, *sizes)
    lines = after(
        jnp.concatenate(lines), beside[0][1], across[0][0], other[1], far_upper, down_pair[1]
    )
    lines = [lines] + plane_rest([lines], *sizes)
    near = [pair for pairs in zip(beside, across) for pair in pairs]
    lines += [
        group_xor(lines[0], group_count, 1),
        *[group_xor(v, group_count, 1) for v in lines[1:]],
    ]
    down_rest = plane_rest([jnp.concatenate(down_pair)], *sizes)
    far_lower = tensor_xor(after(lower, far_upper), tensor_count, 2)
    upper_pair = plane_pair(far_upper, *sizes)
    middle, second = attend(
        segment,
        projected,
        lines,
        (0, KEY_VALUE_HEADS),
        (hidden_in, norm_gains[1], w_out),
    )
    far = after(second, far_lower, upper_pair[1], *down_rest, across[0][1])
    far = tensor_xor(far, tensor_count, 1)
    upper_rest = plane_rest([jnp.concatenate([after(v, second) for v in upper_pair])], *sizes)
    lower_pair = plane_pair(far_lower, *sizes)
    lower_rest = plane_rest([jnp.concatenate(lower_pair)], *sizes)
    late = zip(
        upper_pair + halves_of(upper_rest),
        lower_pair + halves_of(lower_rest),
        down_pair + halves_of(down_rest),
    )
    late = list(late)
    beside = group_xor(second, group_count, 1)
    near = merge_pieces([mine, other] + near)
    late = merge_pieces(late)
    own_early = feed_forward(second, beside, near, [], jnp.float32)
    far_beside = group_xor(
        after(far, own_early[0], lower_pair[1], *upper_rest), group_count, 1
    )
    far_early = feed_forward(
        far, far_beside, near, [], jnp.float32, [*own_early, *lower_rest]
    )
    outgoing = select_pages(projected, page_dest[:, 0], group_count, [far])
    far_sum, far_beside_sum = feed_forward(
        far, far_beside, late, far_early, jnp.bfloat16, [outgoing[0]]
    )
    far_sum = far_sum + group_xor(far_beside_sum, group_count, 1).astype(jnp.float32)
    far_sum = far_sum.astype(jnp.bfloat16)
    returned = tensor_xor(far_sum, tensor_count, 1)
    received = [outgoing[0], group_xor(after(outgoing[1], far_sum), group_count, 1)]
    received += [
        group_xor(outgoing[bits], group_count, bits) for bits in range(2, group_count)
    ]
    own_sum, beside_sum = feed_forward(
        after(second, far_sum, received[1]), beside, late, [*own_early, middle], jnp.bfloat16
    )
    received = place_pages(received)
    own_beside = group_xor(after(beside_sum, received), group_count, 1)
    hidden_out = add_rows(own_sum, own_beside, after(returned, received))
    pages = received.reshape(group_count, CAP, -1, received.shape[2])
    return (hidden_out, pages[None, None])


def solution(mesh):
    return jax.shard_map(
        on_device,
        mesh=mesh,
        in_specs=(
            P(("group", "tensor"), None),
            P(("group", "tensor"), None),
            P(),
            P(),
            P(),
            P(None, None, "tensor"),
            P("tensor", None),
            P("group", "tensor", None),
            P(),
            P(("group", "tensor"), None),
        ),
        out_specs=(P(("group", "tensor"), None), P("group", "tensor", None, None, None, None)),
        check_vma=False,
    )
```

```python
import functools

import jax
import jax.numpy as jnp
from jax import lax
from jax.experimental import pallas as pl
from jax.experimental.pallas import tpu as pltpu
from jax.sharding import PartitionSpec as P

QUERY_HEADS = 16
KEY_VALUE_HEADS = 8
HEAD_DIMENSION = 96
PREFIX_TOKENS = 1024
CAP = 8


ROPE_BASE = 100000.0
EPSILON = 1e-05
NEGATIVE_FILLER = -1e30
LOG2_E = 1.4426950408889634


Z_SIZE = 4


def tensor_xor(value, tensor_count, z_bits):
    width = tensor_count // Z_SIZE
    pairs = [
        (z * width + y, (z ^ z_bits) * width + y) for z in range(Z_SIZE) for y in range(width)
    ]
    return lax.ppermute(value, "tensor", pairs)


def tensor_turn(value, tensor_count, step):
    width = tensor_count // Z_SIZE
    pairs = [
        (z * width + y, z * width + (y + step) % width)
        for z in range(Z_SIZE)
        for y in range(width)
    ]
    return lax.ppermute(value, "tensor", pairs)


def group_xor(value, group_count, bits):
    return lax.ppermute(value, "group", [(g, g ^ bits) for g in range(group_count)])


def own_quarter(block, prefix_owner, group_count):
    group = lax.axis_index("group")
    owner = prefix_owner[lax.axis_index("tensor")]
    rows = block.shape[0] // group_count
    quarter = block[:rows]
    for bits in range(1, group_count):
        came = group_xor(block[bits * rows : (bits + 1) * rows], group_count, bits)
        quarter = jnp.where(owner == (group ^ bits), came, quarter)
    return quarter


HBM = pl.BlockSpec(memory_space=pltpu.HBM)
ANYWHERE = pl.BlockSpec(memory_space=pl.ANY)


def whole(array):
    return pl.BlockSpec(array.shape, lambda *_: (0,) * len(array.shape))


def wholes(arrays):
    return [whole(array) for array in arrays]


def after(value, *earlier):
    return lax.optimization_barrier((value, *earlier))[0]


def swap_in_plane(value, x_core, group_count, tensor_count):
    pairs = []
    for group in range(group_count):
        for place in range(tensor_count):
            over_x = group % 2 == x_core
            target = (group ^ 2, place) if over_x else (group, place ^ 1)
            pairs.append((group * tensor_count + place, target[0] * tensor_count + target[1]))
    return lax.ppermute(value, ("group", "tensor"), pairs)


def plane_pair(value, group_count, tensor_count):
    if tensor_count != 2 * Z_SIZE:
        return [value, group_xor(value, group_count, 2)]
    return [value, swap_in_plane(value, 0, group_count, tensor_count)]


def plane_rest(pair, group_count, tensor_count):
    width = tensor_count // Z_SIZE
    if width != 2:
        return [tensor_turn(v, tensor_count, step) for step in range(1, width) for v in pair]
    return [swap_in_plane(v, 1, group_count, tensor_count) for v in pair]


def pack_kernel(side, w_in, w_down, inward, down, *halves):
    part = w_in.shape[2] // 2
    columns = pl.ds(pl.multiple_of(side[0] * part, part), part)
    for half in range(2):
        inward[:, half * part : (half + 1) * part] = w_in[half, :, columns]
    for block in range(down.shape[0] // part):
        down[block * part : (block + 1) * part, :] = w_down[
            columns, block * 2 * part : (block + 1) * 2 * part
        ]
    for step, out in enumerate(halves):

        @pl.when(pl.program_id(0) == step)
        def _():
            out[...] = inward[...]


def join_piece(gate, up, down):
    width = 2 * gate.shape[1]
    blocks = [down[:, at : at + width] for at in range(0, down.shape[1], width)]
    return jnp.concatenate([gate, up], axis=1), jnp.concatenate(blocks)


def split_piece(piece):
    inward, down = piece
    part = inward.shape[1] // 2
    blocks = [down[at : at + part] for at in range(0, down.shape[0], part)]
    return inward[:, :part], inward[:, part:], jnp.concatenate(blocks, axis=1)


def own_piece(w_in, w_down, side, halved):
    core = lax.axis_index("group") % 2
    depth, part = w_in.shape[1], w_in.shape[2] // 4
    if part % 128:
        start = (core * 2 + side) * part
        inward, down = join_piece(
            lax.dynamic_slice_in_dim(w_in[0], start, part, 1),
            lax.dynamic_slice_in_dim(w_in[1], start, part, 1),
            lax.dynamic_slice_in_dim(w_down, start, part, 0),
        )
        return [inward, down, inward[: depth // 2], inward[depth // 2 :]]
    shapes = [(depth, 2 * part), (depth // 2, 2 * part)]
    halves = [(depth // 2, 2 * part)] * (2 if halved else 0)
    return pl.pallas_call(
        pack_kernel,
        grid_spec=pltpu.PrefetchScalarGridSpec(
            num_scalar_prefetch=1,
            grid=(2,),
            in_specs=[
                pl.BlockSpec((2, depth // 2, 2 * part), lambda i, at: (0, i, at[1])),
                pl.BlockSpec((2 * part, depth // 2), lambda i, at: (at[1], i)),
            ],
            out_specs=[
                pl.BlockSpec((rows // 2, columns), lambda i, at: (i, 0)) for rows, columns in shapes
            ]
            + [pl.BlockSpec(shape, lambda i, at: (0, 0)) for shape in halves],
        ),
        out_shape=[jax.ShapeDtypeStruct(shape, w_in.dtype) for shape in shapes + halves],
        compiler_params=pltpu.CompilerParams(vmem_limit_bytes=60 << 20),
    )(jnp.stack([side, core]).astype(jnp.int32), w_in, w_down)


def halves_of(arrays):
    return [(array, half) for array in arrays for half in range(2)]


def block_of(chunk):
    if not isinstance(chunk, tuple):
        return whole(chunk)
    array, half = chunk
    return pl.BlockSpec((array.shape[0] // 2, array.shape[1]), lambda *_: (half, 0))


def rows_of(chunk):
    if not isinstance(chunk, tuple):
        return chunk
    array, half = chunk
    return jnp.split(array, 2)[half]


def merge_pieces(pieces):
    count = max(1, 128 // (pieces[0][0].shape[1] // 2))
    if count == 1:
        return pieces
    merged = []
    for at in range(0, len(pieces), count):
        taken = [[rows_of(chunk) for chunk in p] for p in pieces[at : at + count]]
        joined = [(jnp.concatenate(p[:-1]), p[-1]) for p in taken]
        gates, ups, downs = zip(*[split_piece(p) for p in joined])
        merged.append(
            join_piece(
                jnp.concatenate(gates, axis=1),
                jnp.concatenate(ups, axis=1),
                jnp.concatenate(downs),
            )
        )
    return merged


def rms_norm(inputs, gain_row):
    floated = inputs.astype(jnp.float32)
    return (
        floated
        * lax.rsqrt(jnp.mean(floated * floated, axis=-1, keepdims=True) + EPSILON)
        * gain_row
    )


def positions(segment):
    row_number = segment.shape[0]
    row_index = jnp.arange(row_number, dtype=jnp.int32)
    same_request = segment[:, None] == segment[None, :]
    first_row = jnp.min(jnp.where(same_request, row_index[None, :], row_number), axis=1)
    return PREFIX_TOKENS + row_index - first_row


def rotary_tables(locate_position, width):
    half_dim = HEAD_DIMENSION // 2
    frequency = ROPE_BASE ** (-jnp.arange(half_dim, dtype=jnp.float32) / half_dim)
    angles = locate_position.astype(jnp.float32)[:, None] * frequency[None, :]
    cosine, sine = jnp.cos(angles), jnp.sin(angles)
    heads = width // HEAD_DIMENSION
    return jnp.tile(cosine, (1, 2 * heads)), jnp.tile(
        jnp.concatenate([-sine, sine], axis=1), (1, heads)
    )


def project_kernel(hidden, gain, weight, cosine, sine, *rest):
    out, normed = rest[-2:]
    step = pl.program_id(0)
    width = weight.shape[1]
    rotated_steps = (QUERY_HEADS + KEY_VALUE_HEADS) * HEAD_DIMENSION // width

    @pl.when(step == 0)
    def _():
        normed[...] = rms_norm(hidden[...], gain[...]).astype(jnp.bfloat16)

    projected = jnp.dot(normed[...], weight[...], preferred_element_type=jnp.float32)

    @pl.when(step < rotated_steps)
    def _():
        half_dim = HEAD_DIMENSION // 2
        lane = lax.broadcasted_iota(jnp.int32, projected.shape, 1)
        swapped = jnp.where(
            lane % HEAD_DIMENSION < half_dim,
            pltpu.roll(projected, width - half_dim, 1),
            pltpu.roll(projected, half_dim, 1),
        )
        heads = width // HEAD_DIMENSION
        cosines = jnp.concatenate([cosine[...]] * heads, axis=1)
        sines = jnp.concatenate([sine[...]] * heads, axis=1)
        out[...] = (projected * cosines + swapped * sines).astype(jnp.bfloat16)

    @pl.when(step >= rotated_steps)
    def _():
        out[...] = projected.astype(jnp.bfloat16)


def project(hidden_in, gain_row, weight, locate_position, earlier):
    rows, depth = hidden_in.shape
    columns = weight.shape[1]
    width = 8 * HEAD_DIMENSION
    cosine, sine = rotary_tables(locate_position, HEAD_DIMENSION)
    return pl.pallas_call(
        project_kernel,
        grid=(columns // width,),
        in_specs=[
            whole(hidden_in),
            whole(gain_row[None, :]),
            pl.BlockSpec((depth, width), lambda i: (0, i)),
            whole(cosine),
            whole(sine),
        ]
        + [pl.BlockSpec(memory_space=pl.ANY)] * len(earlier),
        out_specs=pl.BlockSpec((rows, width), lambda i: (0, i)),
        out_shape=jax.ShapeDtypeStruct((rows, columns), jnp.bfloat16),
        scratch_shapes=[pltpu.VMEM((rows, depth), jnp.bfloat16)],
        compiler_params=pltpu.CompilerParams(vmem_limit_bytes=60 << 20),
        cost_estimate=pl.CostEstimate(
            flops=2 * rows * depth * columns,
            bytes_accessed=2 * depth * columns,
            transcendentals=0,
        ),
    )(hidden_in, gain_row[None, :], weight, cosine, sine, *earlier)


def head_columns(index):
    return slice(index * HEAD_DIMENSION, (index + 1) * HEAD_DIMENSION)


def attention_kernel(piece_count, heads, row_ids, column_ids, projected, *rest):
    pieces, out, joined, semaphores = rest[:piece_count], *rest[-3:]
    rows = projected.shape[0]
    repeats = QUERY_HEADS // KEY_VALUE_HEADS
    first, count = heads
    width = count * HEAD_DIMENSION
    key_value_width = KEY_VALUE_HEADS * HEAD_DIMENSION
    copies, at = [], 0
    for index, piece in enumerate(pieces):
        for side in range(2):
            start = side * key_value_width + first * HEAD_DIMENSION
            source = piece.at[:, pl.ds(start, width)]
            target = joined.at[pl.ds(at, piece.shape[0]), pl.ds(side * width, width)]
            copies.append(pltpu.make_async_copy(source, target, semaphores.at[2 * index + side]))
        at += piece.shape[0]
    for copy in copies:
        copy.start()
    for side in range(2):
        start = (QUERY_HEADS + side * KEY_VALUE_HEADS + first) * HEAD_DIMENSION
        joined[at : at + rows, side * width : (side + 1) * width] = projected[
            :, start : start + width
        ]
    row_index = lax.broadcasted_iota(jnp.int32, (rows, rows), 0)
    column_index = lax.broadcasted_iota(jnp.int32, (rows, rows), 1)
    allowed = (row_ids[...] == column_ids[...]) & (column_index <= row_index)
    allowed = jnp.concatenate([allowed] * repeats, axis=0)
    scale = HEAD_DIMENSION ** (-0.5) * LOG2_E
    for copy in copies:
        copy.wait()
    for head in range(count):
        queries = jnp.concatenate(
            [projected[:, head_columns((first + head) * repeats + g)] for g in range(repeats)],
            axis=0,
        )
        scores = lax.dot_general(
            queries,
            joined[:, head_columns(head)],
            (((1,), (1,)), ((), ())),
            preferred_element_type=jnp.float32,
        )
        scores = jnp.concatenate(
            [scores[:, :at], jnp.where(allowed, scores[:, at:], NEGATIVE_FILLER)], axis=1
        )
        top = jnp.max(scores, axis=1, keepdims=True)
        weights = jnp.exp2((scores - top) * scale)
        total = jnp.sum(weights, axis=1, keepdims=True)
        summed = jnp.dot(
            weights.astype(jnp.bfloat16),
            joined[:, head_columns(count + head)],
            preferred_element_type=jnp.float32,
        )
        attended = (summed / total).astype(jnp.bfloat16)
        for g in range(repeats):
            out[:, head_columns(head * repeats + g)] = attended[g * rows : (g + 1) * rows]


def last_attention_kernel(
    piece_count, heads, row_ids, column_ids, projected, hidden, gain, *rest
):
    pieces, w_out = rest[:piece_count], rest[piece_count]
    middle, second, joined, semaphores, out, weight, semaphore = rest[-7:]
    fetch = pltpu.make_async_copy(w_out, weight, semaphore)
    fetch.start()
    attention_kernel(
        piece_count, heads, row_ids, column_ids, projected, *pieces, out, joined, semaphores
    )
    fetch.wait()
    added = jnp.dot(out[...], weight[...], preferred_element_type=jnp.float32)
    middle[...] = (hidden[...].astype(jnp.float32) + added).astype(jnp.bfloat16)
    second[...] = rms_norm(middle[...], gain[...]).astype(jnp.bfloat16)


def attend(segment, projected, pieces, heads, rest=None):
    rows = projected.shape[0]
    key_count = rows + sum(piece.shape[0] for piece in pieces)
    width = heads[1] * HEAD_DIMENSION
    columns = width * QUERY_HEADS // KEY_VALUE_HEADS
    resident = [segment[:, None], segment[None, :], projected]
    remote = list(pieces)
    kernel = attention_kernel
    out = [jax.ShapeDtypeStruct((rows, columns), jnp.bfloat16)]
    scratch = [
        pltpu.VMEM((key_count, 2 * width), jnp.bfloat16),
        pltpu.SemaphoreType.DMA((2 * len(pieces),)),
    ]
    if rest is not None:
        hidden_in, gain_row, w_out = rest
        resident += [hidden_in, gain_row[None, :]]
        remote.append(w_out)
        kernel = last_attention_kernel
        out = [jax.ShapeDtypeStruct(hidden_in.shape, jnp.bfloat16)] * 2
        scratch += [
            pltpu.VMEM((rows, columns), jnp.bfloat16),
            pltpu.VMEM(w_out.shape, jnp.bfloat16),
            pltpu.SemaphoreType.DMA,
        ]
    return pl.pallas_call(
        functools.partial(kernel, len(pieces), heads),
        grid=(1,),
        in_specs=wholes(resident) + [HBM] * len(remote),
        out_specs=wholes(out),
        out_shape=out,
        scratch_shapes=scratch,
        compiler_params=pltpu.CompilerParams(vmem_limit_bytes=60 << 20),
    )(*resident, *remote)


def feed_forward_kernel(chunks, piece_count, carry_count, left, right, *rest):
    weights = rest[: chunks * piece_count]
    carries = rest[chunks * piece_count : chunks * piece_count + carry_count]
    left_out, right_out, tokens, acts = rest[-4:]
    rows, depth = left.shape
    part = weights[0].shape[1] // 2
    tokens[:rows, :] = left[...]
    tokens[rows:, :] = right[...]
    for index in range(piece_count):
        both, at = 0.0, 0
        for weight in weights[chunks * index : chunks * (index + 1) - 1]:
            columns = slice(at, at + weight.shape[0])
            both += jnp.dot(
                tokens[:, columns], weight[...], preferred_element_type=jnp.float32
            )
            at += weight.shape[0]
        gate, up = both[:, :part], both[:, part:]
        acts[:, index * part : (index + 1) * part] = (gate / (1.0 + jnp.exp(-gate)) * up).astype(
            jnp.bfloat16
        )
    for block in range(depth // (2 * part)):
        columns = slice(block * 2 * part, (block + 1) * 2 * part)
        weight = jnp.concatenate(
            [v[block * part : (block + 1) * part, :] for v in weights[chunks - 1 :: chunks]]
        )
        sums = jnp.dot(acts[...], weight, preferred_element_type=jnp.float32)
        for side, out in enumerate((left_out, right_out)):
            found = sums[side * rows : (side + 1) * rows]
            for carry in carries[side::2]:
                found += carry[:, columns].astype(jnp.float32)
            out[:, columns] = found.astype(out.dtype)


def feed_forward(left, right, pieces, carries, right_dtype, earlier=()):
    rows, depth = left.shape
    part = pieces[0][0].shape[1] // 2
    chunks = [chunk for piece in pieces for chunk in piece]
    blocks = [block_of(chunk) for chunk in chunks]
    chunks = [chunk[0] if isinstance(chunk, tuple) else chunk for chunk in chunks]
    out = [jax.ShapeDtypeStruct((rows, depth), dtype) for dtype in (jnp.float32, right_dtype)]
    return pl.pallas_call(
        functools.partial(feed_forward_kernel, len(pieces[0]), len(pieces), len(carries)),
        grid=(1,),
        in_specs=[
            *wholes([left, right]),
            *blocks,
            *wholes(carries),
            *[ANYWHERE] * len(earlier),
        ],
        out_specs=wholes(out),
        out_shape=out,
        scratch_shapes=[
            pltpu.VMEM((2 * rows, depth), jnp.bfloat16),
            pltpu.VMEM((2 * rows, part * len(pieces)), jnp.bfloat16),
        ],
        compiler_params=pltpu.CompilerParams(vmem_limit_bytes=32 << 20),
    )(left, right, *chunks, *carries, *earlier)


def add_rows(first, *others):
    arrays = [first, *others]
    def kernel(*refs):
        refs[-1][...] = sum(ref[...].astype(jnp.float32) for ref in refs[:-1]).astype(jnp.bfloat16)

    return pl.pallas_call(
        kernel,
        grid=(1,),
        in_specs=wholes(arrays),
        out_specs=whole(first),
        out_shape=jax.ShapeDtypeStruct(first.shape, jnp.bfloat16),
    )(*arrays)


def select_kernel(group_count, table, projected, *rest):
    outs = rest[-group_count:]
    page_rows = outs[0].shape[0] // CAP
    columns = outs[0].shape[1]
    for index in range(group_count * CAP):
        page = table[index]
        start = pl.multiple_of(jnp.maximum(page, 0) * page_rows, page_rows)
        rows = projected[pl.ds(start, page_rows), columns:]
        slot = index % CAP
        outs[index // CAP][slot * page_rows : (slot + 1) * page_rows, :] = jnp.where(
            page >= 0, rows, jnp.zeros_like(rows)
        )


def select_pages(projected, destination, group_count, earlier):
    page_count = destination.shape[0]
    page_rows = projected.shape[0] // page_count
    group = lax.axis_index("group")
    same = destination[:, None] == destination[None, :]
    page = jnp.arange(page_count, dtype=jnp.int32)
    rank = jnp.sum(same & (page[None, :] < page[:, None]), axis=1, dtype=jnp.int32)
    slot = (destination ^ group) * CAP + rank
    chosen = slot[None, :] == jnp.arange(group_count * CAP, dtype=jnp.int32)[:, None]
    table = jnp.max(jnp.where(chosen, page[None, :], -1), axis=1)
    columns = projected.shape[1] // 2
    out = [jax.ShapeDtypeStruct((CAP * page_rows, columns), projected.dtype)] * group_count
    return pl.pallas_call(
        functools.partial(select_kernel, group_count),
        grid_spec=pltpu.PrefetchScalarGridSpec(
            num_scalar_prefetch=1,
            grid=(1,),
            in_specs=[whole(projected)] + [ANYWHERE] * len(earlier),
            out_specs=wholes(out),
        ),
        out_shape=out,
        compiler_params=pltpu.CompilerParams(vmem_limit_bytes=16 << 20),
    )(table, projected, *earlier)


def place_kernel(group, *rest):
    *received, out = rest
    for bits, block in enumerate(received):
        out[group[0] ^ bits] = block[...]


def place_pages(received):
    out = jax.ShapeDtypeStruct((len(received), *received[0].shape), received[0].dtype)
    return pl.pallas_call(
        place_kernel,
        grid_spec=pltpu.PrefetchScalarGridSpec(
            num_scalar_prefetch=1,
            grid=(1,),
            in_specs=wholes(received),
            out_specs=whole(out),
        ),
        out_shape=out,
    )(lax.axis_index("group")[None].astype(jnp.int32), *received)


def on_device(
    hidden_in,
    request_ids,
    norm_gains,
    query_key_value_weight,
    w_out,
    w_in,
    w_down,
    prefix_cache,
    prefix_owner,
    page_dest,
):
    group_count, tensor_count = lax.axis_size("group"), lax.axis_size("tensor")
    sizes = (group_count, tensor_count)
    turns = range(1, tensor_count // Z_SIZE)
    segment = request_ids[0]
    quarter = own_quarter(prefix_cache[0], prefix_owner, group_count)
    across = lax.axis_index("group") // 2
    *mine, upper, lower = own_piece(w_in, w_down, across, True)
    far_down = tensor_xor(mine[1], tensor_count, 2)
    beside = [[tensor_turn(v, tensor_count, step) for v in mine] for step in turns]
    along_z = [tensor_xor(quarter, tensor_count, bits) for bits in range(1, Z_SIZE)]
    projected = project(
        after(hidden_in, mine[0], quarter),
        norm_gains[0],
        query_key_value_weight,
        positions(after(segment, quarter)),
        [],
    )
    line = after(jnp.concatenate([quarter] + along_z), projected, far_down)
    other = own_piece(w_in, w_down, after(1 - across, projected), False)[:2]
    far_upper = tensor_xor(after(upper, line), tensor_count, 2)
    lines = plane_pair(line, *sizes)
    across = [[group_xor(v, group_count, 2) for v in pair] for pair in beside]
    down_pair = plane_pair(far_down, *sizes)
    lines = after(
        jnp.concatenate(lines), beside[0][1], across[0][0], other[1], far_upper, down_pair[1]
    )
    lines = [lines] + plane_rest([lines], *sizes)
    near = [pair for pairs in zip(beside, across) for pair in pairs]
    lines += [
        group_xor(lines[0], group_count, 1),
        *[group_xor(v, group_count, 1) for v in lines[1:]],
    ]
    down_rest = plane_rest([jnp.concatenate(down_pair)], *sizes)
    far_lower = tensor_xor(after(lower, far_upper), tensor_count, 2)
    upper_pair = plane_pair(far_upper, *sizes)
    middle, second = attend(
        segment,
        projected,
        lines,
        (0, KEY_VALUE_HEADS),
        (hidden_in, norm_gains[1], w_out),
    )
    far = after(second, far_lower, upper_pair[1], *down_rest, across[0][1])
    far = tensor_xor(far, tensor_count, 1)
    upper_rest = plane_rest([jnp.concatenate([after(v, second) for v in upper_pair])], *sizes)
    lower_pair = plane_pair(far_lower, *sizes)
    lower_rest = plane_rest([jnp.concatenate(lower_pair)], *sizes)
    late = zip(
        upper_pair + halves_of(upper_rest),
        lower_pair + halves_of(lower_rest),
        down_pair + halves_of(down_rest),
    )
    late = list(late)
    beside = group_xor(second, group_count, 1)
    near = merge_pieces([mine, other] + near)
    late = merge_pieces(late)
    own_early = feed_forward(second, beside, near, [], jnp.float32)
    far_beside = group_xor(
        after(far, own_early[0], lower_pair[1], *upper_rest), group_count, 1
    )
    far_early = feed_forward(
        far, far_beside, near, [], jnp.float32, [*own_early, *lower_rest]
    )
    outgoing = select_pages(projected, page_dest[:, 0], group_count, [far])
    far_sum, far_beside_sum = feed_forward(
        far, far_beside, late, far_early, jnp.bfloat16, [outgoing[0]]
    )
    far_sum = far_sum + group_xor(far_beside_sum, group_count, 1).astype(jnp.float32)
    far_sum = far_sum.astype(jnp.bfloat16)
    returned = tensor_xor(far_sum, tensor_count, 1)
    received = [outgoing[0], group_xor(after(outgoing[1], far_sum), group_count, 1)]
    received += [
        group_xor(outgoing[bits], group_count, bits) for bits in range(2, group_count)
    ]
    own_sum, beside_sum = feed_forward(
        after(second, far_sum, received[1]), beside, late, [*own_early, middle], jnp.bfloat16
    )
    own_beside = group_xor(after(beside_sum, *received[2:]), group_count, 1)
    received = place_pages(received)
    hidden_out = add_rows(own_sum, own_beside, after(returned, received))
    pages = received.reshape(group_count, CAP, -1, received.shape[2])
    return (hidden_out, pages[None, None])


def solution(mesh):
    return jax.shard_map(
        on_device,
        mesh=mesh,
        in_specs=(
            P(("group", "tensor"), None),
            P(("group", "tensor"), None),
            P(),
            P(),
            P(),
            P(None, None, "tensor"),
            P("tensor", None),
            P("group", "tensor", None),
            P(),
            P(("group", "tensor"), None),
        ),
        out_specs=(P(("group", "tensor"), None), P("group", "tensor", None, None, None, None)),
        check_vma=False,
    )
```
